32 devices in a mesh: rad: 8 (over z, x), src: 4 (over y, core).
Axes of the slice: x: 2, y: 2, z: 4, core: 2. Of those that a mesh axis runs over, the one named last changes fastest.
Arguments:
- slab: bfloat16 [1024, 256, 512], P('rad', 'src'), may hold values from -6 to 6
- radius_factor: bfloat16 [1024, 256], P('rad'), may hold values from -2.5 to 2.5
- height_factor: bfloat16 [512, 256], P('src'), may hold values from -2.5 to 2.5
- source_factor: bfloat16 [256, 256], P('src'), may hold values from -2.5 to 2.5
Outputs:
- grad_radius: float32 [1024, 256], P('rad')
- grad_height: float32 [512, 256], P('src')
- grad_source: float32 [256, 256], P('src')
The draws below stay inside these ranges and needn't reach their ends.
All inputs are finite; a program needn't handle non-finite values.
Results may differ from the reference program's by a relative error of at most 0.00046.
Values may be sent and summed in bfloat16 or wider, within the bound.
No kernel may reach another device: no remote copies, remote signals or barrier semaphores. Data moves between devices by JAX's collectives and lax.ppermute only.
A program may use at most 128 MiB of HBM per device.

```python
import jax
import jax.numpy as jnp
from jax import lax

H = 512
K = 256
R_DEV = 128
R = 1024
S = 256


def spiked(entries, rng, source, target, blocks, factor):
    def block_of(position):
        return (jnp.arange(entries.shape[position]) // (entries.shape[position] // blocks)).reshape((-1,) + (1,) * (entries.ndim - 1 - position))

    one_side = jax.random.permutation(rng, blocks)[block_of(target)]
    far = (block_of(target) + blocks // 2) % blocks
    return jnp.where((block_of(source) == one_side) | (block_of(source) == far), factor * entries, entries)


def block_levels(stream_key, dims, split, smallest, largest):
    loudness, own = 1.0, jax.random.fold_in(stream_key, 6)
    for position, blocks in split:
        steps = jnp.exp(jax.random.uniform(jax.random.fold_in(own, position), (blocks,), jnp.float32, smallest / len(split), largest / len(split)))
        loudness = loudness * jnp.repeat(steps, dims[position] // blocks).reshape([-1 if axis == position else 1 for axis in range(len(dims))])
    return loudness


def scatter_about(own_key, shape, spread, reach, shards=(), kind=jnp.bfloat16):
    array = jax.random.normal(own_key, shape, jnp.float32) * spread
    if len(shards) > 0:
        array = block_levels(own_key, shape, shards, -0.22, 0.18) * array
    return jnp.clip(array, min=-reach, max=reach).astype(kind)


def noise_with(stream_key, shape, width, reach, cuts, heavy, dtype=jnp.bfloat16):
    entries = width * jax.random.normal(stream_key, shape, jnp.float32)
    if cuts:
        entries = entries * block_levels(stream_key, shape, cuts, -0.22, 0.18)
    return jnp.clip(spiked(entries, jax.random.fold_in(stream_key, 3), *heavy), -reach, reach).astype(dtype)


def setup_inputs(seed: int = 0) -> dict:
    splits = jax.random.split(jax.random.key(seed), 5)
    slab = noise_with(splits[0], (R, S, H), 1.0, 6.0, ((0, 8), (1, 4)), (0, 2, 8, 2.0))
    radius_factor = scatter_about(splits[1], (R, K), 0.4, 2.5, ((0, 8),))
    height_factor = scatter_about(splits[2], (H, K), 0.4, 2.5, ((0, 4),))
    source_factor = scatter_about(splits[3], (S, K), 0.4, 2.5, ((0, 4),))
    return dict(slab=slab, radius_factor=radius_factor, height_factor=height_factor, source_factor=source_factor)


def reference(slab, radius_factor, height_factor, source_factor):
    src_f = source_factor.astype(jnp.float32)
    hgt_f = height_factor.astype(jnp.float32)
    kr_bc = (src_f[:, None, :] * hgt_f[None, :, :]).astype(jnp.bfloat16).reshape(S * H, K)
    blocks = slab.reshape(R // R_DEV, R_DEV, S * H)
    a_blocks = radius_factor.reshape(R // R_DEV, R_DEV, K)

    def advance(carry, item):
        grad_hgt, grad_src = carry
        rows, a_rows = item
        rebuilt = lax.dot_general(a_rows, kr_bc, (((1,), (1,)), ((), ())), preferred_element_type=jnp.float32)
        residual = (rebuilt - rows.astype(jnp.float32)).astype(jnp.bfloat16)
        err_rows = residual.reshape(R_DEV * S, H)
        projected = jnp.dot(err_rows, height_factor, preferred_element_type=jnp.float32).reshape(R_DEV, S, K)
        a_f = a_rows.astype(jnp.float32)
        part_a = jnp.einsum('rsk,sk->rk', projected, src_f, precision=lax.Precision.HIGHEST)
        grad_src = grad_src + jnp.einsum('rsk,rk->sk', projected, a_f, precision=lax.Precision.HIGHEST)
        kr_ac = (a_f[:, None, :] * src_f[None, :, :]).astype(jnp.bfloat16).reshape(R_DEV * S, K)
        grad_hgt = grad_hgt + lax.dot_general(err_rows, kr_ac, (((0,), (0,)), ((), ())), preferred_element_type=jnp.float32)
        return ((grad_hgt, grad_src), part_a)
    start = (jnp.zeros((H, K), jnp.float32), jnp.zeros((S, K), jnp.float32))
    (grad_hgt, grad_src), parts = lax.scan(advance, start, (blocks, a_blocks))
    grad_radius = parts.reshape(R, K) / jnp.sqrt(jnp.float32(S * H))
    grad_height = grad_hgt / jnp.sqrt(jnp.float32(R * S))
    grad_source = grad_src / jnp.sqrt(jnp.float32(R * H))
    return (grad_radius, grad_height, grad_source)
```

```python
import functools

import jax
import jax.numpy as jnp
from jax import lax
from jax.experimental import pallas as pl
from jax.experimental.pallas import tpu as pltpu
from jax.sharding import PartitionSpec as P

F32 = jnp.float32
BF16 = jnp.bfloat16
F16 = jnp.float16
VMEM_LIMIT = 32 * 1024 * 1024
LANES = 128
TAIL = 16
TOP = 13.0
WHOLE = pl.BlockSpec(memory_space=pltpu.VMEM)


def inside(x):
    return pltpu.with_memory_space_constraint(x, pltpu.VMEM)


def after(x, *others):
    return lax.optimization_barrier((x, *others))[0]


def swap(x, axis, bit):
    return lax.ppermute(x, axis, [(i, i ^ bit) for i in range(lax.axis_size(axis))])


def call(body, outs, args, flops, resident=True, scratch=()):
    return pl.pallas_call(
        body,
        in_specs=[WHOLE] * len(args),
        out_specs=[WHOLE] * len(outs),
        out_shape=[pltpu.VMEM(shape, dtype) for shape, dtype in outs],
        scratch_shapes=scratch,
        compiler_params=pltpu.CompilerParams(vmem_limit_bytes=VMEM_LIMIT),
        cost_estimate=pl.CostEstimate(flops=flops, bytes_accessed=0, transcendentals=0),
    )(*[inside(a) if resident else a for a in args])


def gram(x):
    return lax.dot_general(x, x, (((0,), (0,)), ((), ())), preferred_element_type=F32)


def times(x, m):
    hi = m.astype(BF16)
    lo = (m - hi.astype(F32)).astype(BF16)
    return jnp.dot(x, hi, preferred_element_type=F32) + jnp.dot(x, lo, preferred_element_type=F32)


def prepare(a_ref, b_ref, c_ref, a_out, b_out, cb_out, ga_out):
    h_own = c_ref.shape[0]
    cb_out[0:h_own] = c_ref[...]
    cb_out[h_own:] = b_ref[...]
    a_out[...] = a_ref[...]
    b_out[...] = b_ref[...]
    ga_out[...] = gram(a_ref[...])


def height_terms(offsets, x_ref, a_ref, b_ref, g_ref):
    s_rows, rank = b_ref.shape
    r_rows = a_ref.shape[0]
    rows = r_rows * s_rows
    kr = (a_ref[...][:, None, :] * b_ref[...][None]).reshape(rows, rank)
    if offsets is None:
        x = x_ref[...]
    else:
        width = g_ref.shape[0] // len(offsets)
        me = lax.axis_index("src")
        x = jnp.concatenate(
            [x_ref[:, :, pl.ds(pl.multiple_of((me ^ o) * width, width), width)] for o in offsets], axis=2
        )
    g_ref[...] = lax.dot_general(
        x.reshape(rows, x.shape[2]), kr, (((0,), (0,)), ((), ())), preferred_element_type=F32
    )


def project(scales, n_src, x_ref, a_ref, b_ref, ga_ref, *refs):
    blocks, (pa_ref, ps_ref, ph_ref, heights) = refs[:n_src], refs[n_src:]
    s_rows, rank = b_ref.shape
    r_rows = a_ref.shape[0]
    h_own = blocks[0].shape[0] - s_rows
    me = lax.axis_index("src")
    for o, ref in enumerate(blocks):
        heights[pl.ds(pl.multiple_of((me ^ o) * h_own, h_own), h_own)] = ref[0:h_own]
    x = x_ref[...].reshape(r_rows * s_rows, x_ref.shape[2])
    proj = jnp.dot(x, heights[...], preferred_element_type=F32).reshape(r_rows, s_rows, rank)
    pa = (proj * b_ref[...].astype(F32)[None]).sum(1)
    ps = (proj * a_ref[...].astype(F32)[:, None, :]).sum(0)
    gb_own = gram(b_ref[...])
    gb = gb_own
    for ref in blocks[1:]:
        gb = gb + gram(ref[h_own:])
    gc = gram(heights[...])
    ga = ga_ref[...]
    to_radius, to_height, to_source = scales
    pa_ref[...] = (times(a_ref[...], gb_own * gc) - pa) * to_radius
    ps_ref[...] = (times(b_ref[...], ga * gc) - ps) * to_source
    ph_ref[...] = times(blocks[0][0:h_own], ga * gb) * to_height


def split(v_ref, h_ref, s_ref):
    h_own = h_ref.shape[0]
    h_ref[...] = v_ref[0:h_own]
    s_ref[...] = v_ref[h_own : h_own + s_ref.shape[0]]


def pack(v, e):
    rows = lax.broadcasted_iota(jnp.int32, v.shape, 0)
    return jnp.where(rows < v.shape[0] - TAIL, v * jnp.exp2(TOP - e), e).astype(F16)


def unpack(m):
    e = m[-1:].astype(F32)
    return m.astype(F32) * jnp.exp2(e - TOP), e


def per_device(slab, radius_factor, height_factor, source_factor):
    n_rad, n_src = lax.axis_size("rad"), lax.axis_size("src")
    r_rows, s_rows, width = slab.shape
    h_own, rank = height_factor.shape
    total_r, total_s = r_rows * n_rad, s_rows * n_src
    scales = (
        (total_s * width) ** -0.5,
        (total_r * total_s) ** -0.5,
        (total_r * width) ** -0.5,
    )
    work = 2 * r_rows * s_rows * width * rank
    src_bits = [1 << i for i in range(n_src.bit_length() - 1)]
    rad_bits = [1 << i for i in range(n_rad.bit_length() - 1)]

    a, b, cb, ga = call(
        prepare,
        [((r_rows, rank), BF16), ((s_rows, rank), BF16), ((h_own + s_rows, rank), BF16), ((rank, rank), F32)],
        (radius_factor, source_factor, height_factor),
        work // 2,
        resident=False,
    )
    blocks = {0: cb}
    for bit in reversed(src_bits):
        blocks[bit] = swap(cb, "src", bit)
    if h_own % LANES == 0:
        offsets = list(range(n_src))
        (g_away,) = call(
            functools.partial(height_terms, offsets[1::2]), [((width // 2, rank), F32)], (slab, a, b), work // 2
        )
        g_in = swap(g_away, "src", 1)
        ready = after(a, g_away, *[blocks[bit] for bit in src_bits])
        (g_keep,) = call(
            functools.partial(height_terms, offsets[0::2]), [((width // 2, rank), F32)], (slab, ready, b), work // 2
        )
    else:
        (g,) = call(functools.partial(height_terms, None), [((width, rank), F32)], (slab, a, b), work)
        me = lax.axis_index("src")
        g = jnp.take(g.reshape(n_src, h_own, rank), me ^ jnp.arange(n_src), axis=0)
        g_away, g_keep = (g[i::2].reshape(width // 2, rank) for i in (1, 0))
        g_in = swap(g_away, "src", 1)
    for o in range(1, n_src):
        if o not in blocks:
            low = o & -o
            blocks[o] = swap(after(blocks[o ^ low], g_away), "src", low)
    g = g_keep + g_in
    for bit in src_bits[1:-1]:
        g = g.reshape(-1, 2, h_own, rank)
        g = (g[:, 0] + swap(g[:, 1], "src", bit)).reshape(-1, rank)
    share_in = swap(g[h_own:], "src", src_bits[-1])
    pa, ps, ph = call(
        functools.partial(project, scales, n_src),
        [((r_rows, rank), F32), ((s_rows, rank), F32), ((h_own, rank), F32)],
        (slab, a, b, ga, *[blocks[o] for o in range(n_src)]),
        work,
        scratch=[pltpu.VMEM((width, rank), BF16)],
    )
    ph = ph - (g[:h_own] + share_in) * scales[1]
    v = jnp.concatenate([ph, ps, jnp.zeros((TAIL, rank), F32)], axis=0)
    top = jnp.max(jnp.abs(v), axis=0, keepdims=True)
    e = jnp.clip(jnp.ceil(jnp.log2(jnp.maximum(top, 1e-30))), -100.0, 100.0)
    bits = list(src_bits)
    for i, bit in enumerate(rad_bits):
        m = pack(v, e)
        if bits:
            pa, m = lax.optimization_barrier((pa, m))
            pa = pa + swap(pa, "src", bits.pop(0))
        other, e_other = unpack(swap(m, "rad", bit))
        v, e = unpack(m)
        v = v + other
        e = jnp.maximum(e, e_other) + 1.0
    for bit in bits:
        pa = pa + swap(pa, "src", bit)
    grad_height, grad_source = pl.pallas_call(
        split,
        in_specs=[WHOLE],
        out_specs=[WHOLE] * 2,
        out_shape=[jax.ShapeDtypeStruct((h_own, rank), F32), jax.ShapeDtypeStruct((s_rows, rank), F32)],
    )(inside(v))
    return pa, grad_height, grad_source


def solution(mesh):
    return jax.shard_map(
        per_device,
        mesh=mesh,
        in_specs=(P("rad", "src", None), P("rad", None), P("src", None), P("src", None)),
        out_specs=(P("rad", None), P("src", None), P("src", None)),
        check_vma=False,
    )
```

```python
import functools

import jax
import jax.numpy as jnp
from jax import lax
from jax.experimental import pallas as pl
from jax.experimental.pallas import tpu as pltpu
from jax.sharding import PartitionSpec as P

F32 = jnp.float32
BF16 = jnp.bfloat16
F16 = jnp.float16
VMEM_LIMIT = 32 * 1024 * 1024
LOAD_LIMIT = 54 * 1024 * 1024 + 512 * 1024
LANES = 128
CHUNKS = 8
TAIL = 8
TOP = 13.0
WHOLE = pl.BlockSpec(memory_space=pltpu.VMEM)


def inside(x):
    return pltpu.with_memory_space_constraint(x, pltpu.VMEM)


def after(x, *others):
    return lax.optimization_barrier((x, *others))[0]


def swap(x, axis, bit):
    return lax.ppermute(x, axis, [(i, i ^ bit) for i in range(lax.axis_size(axis))])


def call(body, outs, args, flops, resident=True, scratch=()):
    return pl.pallas_call(
        body,
        in_specs=[WHOLE] * len(args),
        out_specs=[WHOLE] * len(outs),
        out_shape=[pltpu.VMEM(shape, dtype) for shape, dtype in outs],
        scratch_shapes=scratch,
        compiler_params=pltpu.CompilerParams(vmem_limit_bytes=VMEM_LIMIT),
        cost_estimate=pl.CostEstimate(flops=flops, bytes_accessed=0, transcendentals=0),
    )(*[inside(a) if resident else a for a in args])


def gram(x):
    return lax.dot_general(x, x, (((0,), (0,)), ((), ())), preferred_element_type=F32)


def times(x, m):
    hi = m.astype(BF16)
    lo = (m - hi.astype(F32)).astype(BF16)
    return jnp.dot(x, hi, preferred_element_type=F32) + jnp.dot(x, lo, preferred_element_type=F32)


def prepare(a_ref, b_ref, c_ref, a_out, b_out, cb_out, ga_out):
    h_own = c_ref.shape[0]
    cb_out[0:h_own] = c_ref[...]
    cb_out[h_own:] = b_ref[...]
    a_out[...] = a_ref[...]
    b_out[...] = b_ref[...]
    ga_out[...] = gram(a_ref[...])


def height_terms(offsets, x_ref, a_ref, b_ref, g_ref):
    s_rows, rank = b_ref.shape
    r_rows = a_ref.shape[0]
    rows = r_rows * s_rows
    kr = (a_ref[...][:, None, :] * b_ref[...][None]).reshape(rows, rank)
    if offsets is None:
        x = x_ref[...]
    else:
        width = g_ref.shape[0] // len(offsets)
        me = lax.axis_index("src")
        x = jnp.concatenate(
            [x_ref[:, :, pl.ds(pl.multiple_of((me ^ o) * width, width), width)] for o in offsets], axis=2
        )
    g_ref[...] = lax.dot_general(
        x.reshape(rows, x.shape[2]), kr, (((0,), (0,)), ((), ())), preferred_element_type=F32
    )


def load(offsets, x_hbm, a_hbm, b_hbm, c_hbm, x_ref, a_ref, b_ref, cb_ref, ga_ref, g_ref, sems):
    s_rows, rank = b_ref.shape
    r_rows = a_ref.shape[0]
    h_own = c_hbm.shape[0]
    width = g_ref.shape[0] // len(offsets)
    small = [
        pltpu.make_async_copy(a_hbm, a_ref, sems.at[0]),
        pltpu.make_async_copy(b_hbm, b_ref, sems.at[1]),
        pltpu.make_async_copy(c_hbm, cb_ref.at[pl.ds(0, h_own)], sems.at[2]),
        pltpu.make_async_copy(b_hbm, cb_ref.at[pl.ds(h_own, s_rows)], sems.at[3]),
    ]
    rows = r_rows // CHUNKS
    chunks = [
        pltpu.make_async_copy(x_hbm.at[pl.ds(i * rows, rows)], x_ref.at[pl.ds(i * rows, rows)], sems.at[4 + i])
        for i in range(CHUNKS)
    ]
    for copy in small + chunks:
        copy.start()
    for copy in small:
        copy.wait()
    ga_ref[...] = gram(a_ref[...])
    me = lax.axis_index("src")
    at = [pl.ds(pl.multiple_of((me ^ o) * width, width), width) for o in offsets]
    for i, copy in enumerate(chunks):
        mine = pl.ds(i * rows, rows)
        kr = (a_ref[mine][:, None, :] * b_ref[...][None]).reshape(rows * s_rows, rank)
        copy.wait()
        x = jnp.concatenate([x_ref[mine, :, a] for a in at], axis=2).reshape(rows * s_rows, 2 * width)
        part = lax.dot_general(x, kr, (((0,), (0,)), ((), ())), preferred_element_type=F32)
        g_ref[...] = part if i == 0 else g_ref[...] + part


def meet(to_height, g_ref, in_ref, own_ref, mate_ref, cy_ref, ga_ref, keep_ref, away_ref, *top_refs):
    h_own = cy_ref.shape[0]
    s_rows = own_ref.shape[0] - h_own
    sources = pl.ds(h_own, s_rows)
    m = ga_ref[...] * (gram(own_ref[sources]) + gram(mate_ref[sources]))
    g = g_ref[...] + in_ref[...]
    keep_ref[...] = (times(own_ref[0:h_own], m) - g[0:h_own]) * to_height
    away_ref[...] = (times(cy_ref[...], m) - g[h_own:]) * to_height
    for top, part in zip(top_refs, (keep_ref, away_ref)):
        top[...] = column_top(part[...])


def project_four(scales, x_ref, a_ref, b_ref, ga_ref, own_ref, mate_ref, cy_ref, pa_ref, ps_ref, top_ref, heights):
    s_rows, rank = b_ref.shape
    r_rows = a_ref.shape[0]
    h_own = cy_ref.shape[0]
    me = lax.axis_index("src")
    parts = (own_ref[0:h_own], mate_ref[0:h_own], cy_ref[...], mate_ref[h_own + s_rows :])
    for o, part in enumerate(parts):
        heights[pl.ds(pl.multiple_of((me ^ o) * h_own, h_own), h_own)] = part
    x = x_ref[...].reshape(r_rows * s_rows, x_ref.shape[2])
    proj = jnp.dot(x, heights[...], preferred_element_type=F32).reshape(r_rows, s_rows, rank)
    pa = (proj * b_ref[...].astype(F32)[None]).sum(1)
    ps = (proj * a_ref[...].astype(F32)[:, None, :]).sum(0)
    gc = gram(heights[...])
    to_radius, _, to_source = scales
    pa_ref[...] = (times(a_ref[...], gram(b_ref[...]) * gc) - pa) * to_radius
    ps_ref[...] = (times(b_ref[...], ga_ref[...] * gc) - ps) * to_source
    top_ref[...] = column_top(ps_ref[...])


def local_four(slab, radius_factor, height_factor, source_factor, scales):
    r_rows, s_rows, width = slab.shape
    h_own, rank = height_factor.shape
    work = 2 * r_rows * s_rows * width * rank
    cy = swap(height_factor, "src", 2)
    x, a, b, cb, ga, g_away = pl.pallas_call(
        functools.partial(load, (1, 3)),
        in_specs=[pl.BlockSpec(memory_space=pl.ANY)] * 4,
        out_specs=[WHOLE] * 6,
        out_shape=[
            pltpu.VMEM(slab.shape, BF16),
            pltpu.VMEM(radius_factor.shape, BF16),
            pltpu.VMEM(source_factor.shape, BF16),
            pltpu.VMEM((h_own + s_rows, rank), BF16),
            pltpu.VMEM((rank, rank), F32),
            pltpu.VMEM((width // 2, rank), F32),
        ],
        scratch_shapes=[pltpu.SemaphoreType.DMA((4 + CHUNKS,))],
        compiler_params=pltpu.CompilerParams(vmem_limit_bytes=LOAD_LIMIT),
        cost_estimate=pl.CostEstimate(flops=2 * work, bytes_accessed=0, transcendentals=0),
    )(slab, radius_factor, source_factor, height_factor)
    g_in = swap(g_away, "src", 1)
    cby = jnp.concatenate([cb, after(cy, g_away)], axis=0)
    mate = swap(cby, "src", 1)
    (g_keep,) = call(
        functools.partial(height_terms, (0, 2)), [((width // 2, rank), F32)], (x, after(a, cby), b), work // 2
    )
    keep, away, keep_top, away_top = call(
        functools.partial(meet, scales[1]),
        [((h_own, rank), F32), ((h_own, rank), F32), ((1, rank), F32), ((1, rank), F32)],
        (g_keep, g_in, cb, mate, cy, ga),
        work // 8,
    )
    away = pack(padded(away), exponent(away_top))
    share_in, e_in = unpack(swap(away, "src", 2))
    share_in = share_in[:h_own]
    pa, ps, ps_top = call(
        functools.partial(project_four, scales),
        [((r_rows, rank), F32), ((s_rows, rank), F32), ((1, rank), F32)],
        (x, after(a, away), b, ga, cb, mate, cy),
        work,
        scratch=[pltpu.VMEM((width, rank), BF16)],
    )
    return pa, ps, keep + share_in, exponent(jnp.maximum(ps_top, keep_top + jnp.exp2(e_in)))


def project(scales, n_src, x_ref, a_ref, b_ref, ga_ref, *refs):
    blocks, (pa_ref, ps_ref, ph_ref, heights) = refs[:n_src], refs[n_src:]
    s_rows, rank = b_ref.shape
    r_rows = a_ref.shape[0]
    h_own = blocks[0].shape[0] - s_rows
    me = lax.axis_index("src")
    for o, ref in enumerate(blocks):
        heights[pl.ds(pl.multiple_of((me ^ o) * h_own, h_own), h_own)] = ref[0:h_own]
    x = x_ref[...].reshape(r_rows * s_rows, x_ref.shape[2])
    proj = jnp.dot(x, heights[...], preferred_element_type=F32).reshape(r_rows, s_rows, rank)
    pa = (proj * b_ref[...].astype(F32)[None]).sum(1)
    ps = (proj * a_ref[...].astype(F32)[:, None, :]).sum(0)
    gb_own = gram(b_ref[...])
    gb = gb_own
    for ref in blocks[1:]:
        gb = gb + gram(ref[h_own:])
    gc = gram(heights[...])
    ga = ga_ref[...]
    to_radius, to_height, to_source = scales
    pa_ref[...] = (times(a_ref[...], gb_own * gc) - pa) * to_radius
    ps_ref[...] = (times(b_ref[...], ga * gc) - ps) * to_source
    ph_ref[...] = times(blocks[0][0:h_own], ga * gb) * to_height


def local_any(slab, radius_factor, height_factor, source_factor, scales):
    n_src = lax.axis_size("src")
    r_rows, s_rows, width = slab.shape
    h_own, rank = height_factor.shape
    work = 2 * r_rows * s_rows * width * rank
    src_bits = [1 << i for i in range(n_src.bit_length() - 1)]
    a, b, cb, ga = call(
        prepare,
        [((r_rows, rank), BF16), ((s_rows, rank), BF16), ((h_own + s_rows, rank), BF16), ((rank, rank), F32)],
        (radius_factor, source_factor, height_factor),
        work // 2,
        resident=False,
    )
    blocks = {0: cb}
    for bit in reversed(src_bits):
        blocks[bit] = swap(cb, "src", bit)
    if h_own % LANES == 0:
        offsets = list(range(n_src))
        (g_away,) = call(
            functools.partial(height_terms, offsets[1::2]), [((width // 2, rank), F32)], (slab, a, b), work // 2
        )
        g_in = swap(g_away, "src", 1)
        ready = after(a, g_away, *[blocks[bit] for bit in src_bits])
        (g_keep,) = call(
            functools.partial(height_terms, offsets[0::2]), [((width // 2, rank), F32)], (slab, ready, b), work // 2
        )
    else:
        (g,) = call(functools.partial(height_terms, None), [((width, rank), F32)], (slab, a, b), work)
        me = lax.axis_index("src")
        g = jnp.take(g.reshape(n_src, h_own, rank), me ^ jnp.arange(n_src), axis=0)
        g_away, g_keep = (g[i::2].reshape(width // 2, rank) for i in (1, 0))
        g_in = swap(g_away, "src", 1)
    for o in range(1, n_src):
        if o not in blocks:
            low = o & -o
            blocks[o] = swap(after(blocks[o ^ low], g_away), "src", low)
    g = g_keep + g_in
    for bit in src_bits[1:-1]:
        g = g.reshape(-1, 2, h_own, rank)
        g = (g[:, 0] + swap(g[:, 1], "src", bit)).reshape(-1, rank)
    share_in = swap(g[h_own:], "src", src_bits[-1])
    pa, ps, ph = call(
        functools.partial(project, scales, n_src),
        [((r_rows, rank), F32), ((s_rows, rank), F32), ((h_own, rank), F32)],
        (slab, a, b, ga, *[blocks[o] for o in range(n_src)]),
        work,
        scratch=[pltpu.VMEM((width, rank), BF16)],
    )
    ph = ph - (g[:h_own] + share_in) * scales[1]
    return pa, ps, ph, exponent(jnp.maximum(column_top(ph), column_top(ps)))


def split(v_ref, h_ref, s_ref):
    h_own = h_ref.shape[0]
    h_ref[...] = v_ref[0:h_own]
    s_ref[...] = v_ref[h_own : h_own + s_ref.shape[0]]


def exponent(top):
    return jnp.clip(jnp.ceil(jnp.log2(jnp.maximum(top, 1e-30))), -100.0, 100.0)


def pack(v, e):
    rows = lax.broadcasted_iota(jnp.int32, v.shape, 0)
    return jnp.where(rows < v.shape[0] - TAIL, v * jnp.exp2(TOP - e), e).astype(F16)


def unpack(m):
    e = m[-1:].astype(F32)
    return m.astype(F32) * jnp.exp2(e - TOP), e


def padded(*parts):
    return jnp.concatenate([*parts, jnp.zeros((TAIL, parts[0].shape[1]), F32)], axis=0)


def column_top(v):
    return jnp.max(jnp.abs(v), axis=0, keepdims=True)


def per_device(slab, radius_factor, height_factor, source_factor):
    n_rad, n_src = lax.axis_size("rad"), lax.axis_size("src")
    r_rows, s_rows, width = slab.shape
    h_own, rank = height_factor.shape
    total_r, total_s = r_rows * n_rad, s_rows * n_src
    scales = (
        (total_s * width) ** -0.5,
        (total_r * total_s) ** -0.5,
        (total_r * width) ** -0.5,
    )
    src_bits = [1 << i for i in range(n_src.bit_length() - 1)]
    rad_bits = [1 << i for i in range(n_rad.bit_length() - 1)]

    local = local_four if n_src == 4 and h_own % LANES == 0 else local_any
    pa, ps, ph, e = local(slab, radius_factor, height_factor, source_factor, scales)
    v = padded(ph, ps)
    bits = src_bits[::-1]
    for stage in [rad_bits[i : i + 2] for i in range(0, len(rad_bits), 2)]:
        m = pack(v, e)
        others = [0, *stage] if len(stage) == 1 else [0, stage[0], stage[1], sum(stage)]
        terms = [unpack(m)] + [unpack(swap(m, "rad", o)) for o in others[1:]]
        if bits:
            pa = after(pa, m)
            pa = pa + swap(pa, "src", bits.pop(0))
        values = [value for value, _ in terms]
        while len(values) > 1:
            values = [a + b for a, b in zip(values[0::2], values[1::2])]
        (v,) = values
        e = functools.reduce(jnp.maximum, [x for _, x in terms]) + len(stage)
    for bit in bits:
        pa = pa + swap(pa, "src", bit)
    grad_height, grad_source = pl.pallas_call(
        split,
        in_specs=[WHOLE],
        out_specs=[WHOLE] * 2,
        out_shape=[jax.ShapeDtypeStruct((h_own, rank), F32), jax.ShapeDtypeStruct((s_rows, rank), F32)],
    )(inside(after(v, pa)))
    return pa, grad_height, grad_source


def solution(mesh):
    return jax.shard_map(
        per_device,
        mesh=mesh,
        in_specs=(P("rad", "src", None), P("rad", None), P("src", None), P("src", None)),
        out_specs=(P("rad", None), P("src", None), P("src", None)),
        check_vma=False,
    )
```

```python
import functools

import jax
import jax.numpy as jnp
from jax import lax
from jax.experimental import pallas as pl
from jax.experimental.pallas import tpu as pltpu
from jax.sharding import PartitionSpec as P

F32 = jnp.float32
BF16 = jnp.bfloat16
F16 = jnp.float16
VMEM_LIMIT = 32 * 1024 * 1024
LOAD_LIMIT = 54 * 1024 * 1024 + 512 * 1024
LANES = 128
CHUNKS = 8
TAIL = 8
TOP = 13.0
WHOLE = pl.BlockSpec(memory_space=pltpu.VMEM)


def inside(x):
    return pltpu.with_memory_space_constraint(x, pltpu.VMEM)


def after(x, *others):
    return lax.optimization_barrier((x, *others))[0]


def swap(x, axis, bit):
    return lax.ppermute(x, axis, [(i, i ^ bit) for i in range(lax.axis_size(axis))])


def call(body, outs, args, flops, resident=True, scratch=()):
    return pl.pallas_call(
        body,
        in_specs=[WHOLE] * len(args),
        out_specs=[WHOLE] * len(outs),
        out_shape=[pltpu.VMEM(shape, dtype) for shape, dtype in outs],
        scratch_shapes=scratch,
        compiler_params=pltpu.CompilerParams(vmem_limit_bytes=VMEM_LIMIT),
        cost_estimate=pl.CostEstimate(flops=flops, bytes_accessed=0, transcendentals=0),
    )(*[inside(a) if resident else a for a in args])


def gram(x):
    return lax.dot_general(x, x, (((0,), (0,)), ((), ())), preferred_element_type=F32)


def times(x, m):
    hi = m.astype(BF16)
    lo = (m - hi.astype(F32)).astype(BF16)
    return jnp.dot(x, hi, preferred_element_type=F32) + jnp.dot(x, lo, preferred_element_type=F32)


def exponent(top):
    return jnp.clip(jnp.ceil(jnp.log2(jnp.maximum(top, 1e-30))), -100.0, 100.0)


def column_top(v):
    return jnp.max(jnp.abs(v), axis=0, keepdims=True)


def prepare(a_ref, b_ref, c_ref, a_out, b_out, cb_out, ga_out):
    h_own = c_ref.shape[0]
    cb_out[0:h_own] = c_ref[...]
    cb_out[h_own:] = b_ref[...]
    a_out[...] = a_ref[...]
    b_out[...] = b_ref[...]
    ga_out[...] = gram(a_ref[...])


def height_terms(offsets, x_ref, a_ref, b_ref, g_ref):
    s_rows, rank = b_ref.shape
    r_rows = a_ref.shape[0]
    rows = r_rows * s_rows
    kr = (a_ref[...][:, None, :] * b_ref[...][None]).reshape(rows, rank)
    if offsets is None:
        x = x_ref[...]
    else:
        width = g_ref.shape[0] // len(offsets)
        me = lax.axis_index("src")
        x = jnp.concatenate(
            [x_ref[:, :, pl.ds(pl.multiple_of((me ^ o) * width, width), width)] for o in offsets], axis=2
        )
    g_ref[...] = lax.dot_general(
        x.reshape(rows, x.shape[2]), kr, (((0,), (0,)), ((), ())), preferred_element_type=F32
    )


def load(offsets, x_hbm, a_hbm, b_hbm, c_hbm, x_ref, a_ref, b_ref, cb_ref, ga_ref, g_ref, sems):
    s_rows, rank = b_ref.shape
    r_rows = a_ref.shape[0]
    h_own = c_hbm.shape[0]
    width = g_ref.shape[0] // len(offsets)
    small = [
        pltpu.make_async_copy(a_hbm, a_ref, sems.at[0]),
        pltpu.make_async_copy(b_hbm, b_ref, sems.at[1]),
        pltpu.make_async_copy(c_hbm, cb_ref.at[pl.ds(0, h_own)], sems.at[2]),
        pltpu.make_async_copy(b_hbm, cb_ref.at[pl.ds(h_own, s_rows)], sems.at[3]),
    ]
    rows = r_rows // CHUNKS
    chunks = [
        pltpu.make_async_copy(x_hbm.at[pl.ds(i * rows, rows)], x_ref.at[pl.ds(i * rows, rows)], sems.at[4 + i])
        for i in range(CHUNKS)
    ]
    for copy in small + chunks:
        copy.start()
    for copy in small:
        copy.wait()
    ga_ref[...] = gram(a_ref[...])
    me = lax.axis_index("src")
    at = [pl.ds(pl.multiple_of((me ^ o) * width, width), width) for o in offsets]
    for i, copy in enumerate(chunks):
        mine = pl.ds(i * rows, rows)
        kr = (a_ref[mine][:, None, :] * b_ref[...][None]).reshape(rows * s_rows, rank)
        copy.wait()
        x = jnp.concatenate([x_ref[mine, :, a] for a in at], axis=2).reshape(rows * s_rows, 2 * width)
        part = lax.dot_general(x, kr, (((0,), (0,)), ((), ())), preferred_element_type=F32)
        g_ref[...] = part if i == 0 else g_ref[...] + part


def write_message(m_ref, *parts):
    top = functools.reduce(jnp.maximum, [column_top(part) for part in parts])
    e = exponent(top)
    scale = jnp.exp2(TOP - e)
    at = 0
    for part in parts:
        m_ref[at : at + part.shape[0]] = part * scale
        at += part.shape[0]
    m_ref[at:] = jnp.broadcast_to(e, (m_ref.shape[0] - at, e.shape[1]))


def meet(to_height, g_ref, in_ref, own_ref, mate_ref, cy_ref, ga_ref, keep_ref, m_ref):
    h_own = cy_ref.shape[0]
    s_rows = own_ref.shape[0] - h_own
    sources = pl.ds(h_own, s_rows)
    m = ga_ref[...] * (gram(own_ref[sources]) + gram(mate_ref[sources]))
    g = g_ref[...] + in_ref[...]
    keep_ref[...] = (times(own_ref[0:h_own], m) - g[0:h_own]) * to_height
    write_message(m_ref, (times(cy_ref[...], m) - g[h_own:]) * to_height)


def combine(keep_ref, in_ref, ps_ref, m_ref):
    h_own = keep_ref.shape[0]
    share = keep_ref[...] + in_ref[0:h_own] * jnp.exp2(in_ref[h_own : h_own + 1] - TOP)
    write_message(m_ref, share, ps_ref[...])


def radius(to_radius, a_ref, b_ref, gc_ref, slab_ref, pa_ref):
    pa_ref[...] = (times(a_ref[...], gram(b_ref[...]) * gc_ref[...]) - slab_ref[...]) * to_radius


def project_four(to_source, x_ref, a_ref, b_ref, ga_ref, own_ref, mate_ref, cy_ref, pa_ref, ps_ref, gc_ref, heights):
    s_rows, rank = b_ref.shape
    r_rows = a_ref.shape[0]
    h_own = cy_ref.shape[0]
    me = lax.axis_index("src")
    parts = (own_ref[0:h_own], mate_ref[0:h_own], cy_ref[...], mate_ref[h_own + s_rows :])
    for o, part in enumerate(parts):
        heights[pl.ds(pl.multiple_of((me ^ o) * h_own, h_own), h_own)] = part
    x = x_ref[...].reshape(r_rows * s_rows, x_ref.shape[2])
    proj = jnp.dot(x, heights[...], preferred_element_type=F32).reshape(r_rows, s_rows, rank)
    pa_ref[...] = (proj * b_ref[...].astype(F32)[None]).sum(1)
    ps = (proj * a_ref[...].astype(F32)[:, None, :]).sum(0)
    gc = gram(heights[...])
    gc_ref[...] = gc
    ps_ref[...] = (times(b_ref[...], ga_ref[...] * gc) - ps) * to_source


def local_four(slab, radius_factor, height_factor, source_factor, scales):
    r_rows, s_rows, width = slab.shape
    h_own, rank = height_factor.shape
    work = 2 * r_rows * s_rows * width * rank
    cy = swap(height_factor, "src", 2)
    x, a, b, cb, ga, g_away = pl.pallas_call(
        functools.partial(load, (1, 3)),
        in_specs=[pl.BlockSpec(memory_space=pl.ANY)] * 4,
        out_specs=[WHOLE] * 6,
        out_shape=[
            pltpu.VMEM(slab.shape, BF16),
            pltpu.VMEM(radius_factor.shape, BF16),
            pltpu.VMEM(source_factor.shape, BF16),
            pltpu.VMEM((h_own + s_rows, rank), BF16),
            pltpu.VMEM((rank, rank), F32),
            pltpu.VMEM((width // 2, rank), F32),
        ],
        scratch_shapes=[pltpu.SemaphoreType.DMA((4 + CHUNKS,))],
        compiler_params=pltpu.CompilerParams(vmem_limit_bytes=LOAD_LIMIT),
        cost_estimate=pl.CostEstimate(flops=2 * work, bytes_accessed=0, transcendentals=0),
    )(slab, radius_factor, source_factor, height_factor)
    g_in = swap(g_away, "src", 1)
    cby = jnp.concatenate([cb, after(cy, g_away)], axis=0)
    mate = swap(cby, "src", 1)
    (g_keep,) = call(
        functools.partial(height_terms, (0, 2)), [((width // 2, rank), F32)], (x, after(a, cby), b), work // 2
    )
    keep, away = call(
        functools.partial(meet, scales[1]),
        [((h_own, rank), F32), ((h_own + TAIL, rank), F32)],
        (g_keep, g_in, cb, mate, cy, ga),
        work // 8,
    )
    away = away.astype(F16)
    share_in = swap(away, "src", 2)
    pa, ps, gc = call(
        functools.partial(project_four, scales[2]),
        [((r_rows, rank), F32), ((s_rows, rank), F32), ((rank, rank), F32)],
        (x, after(a, away), b, ga, cb, mate, cy),
        work,
        scratch=[pltpu.VMEM((width, rank), BF16)],
    )
    (m,) = call(combine, [((h_own + s_rows + TAIL, rank), F32)], (keep, share_in.astype(F32), ps), work // 32)
    m = m.astype(F16)
    (pa,) = call(
        functools.partial(radius, scales[0]), [((r_rows, rank), F32)], (a, b, gc, after(pa, m)), work // 32
    )
    return pa, m


def project(scales, n_src, x_ref, a_ref, b_ref, ga_ref, *refs):
    blocks, (pa_ref, ps_ref, ph_ref, heights) = refs[:n_src], refs[n_src:]
    s_rows, rank = b_ref.shape
    r_rows = a_ref.shape[0]
    h_own = blocks[0].shape[0] - s_rows
    me = lax.axis_index("src")
    for o, ref in enumerate(blocks):
        heights[pl.ds(pl.multiple_of((me ^ o) * h_own, h_own), h_own)] = ref[0:h_own]
    x = x_ref[...].reshape(r_rows * s_rows, x_ref.shape[2])
    proj = jnp.dot(x, heights[...], preferred_element_type=F32).reshape(r_rows, s_rows, rank)
    pa = (proj * b_ref[...].astype(F32)[None]).sum(1)
    ps = (proj * a_ref[...].astype(F32)[:, None, :]).sum(0)
    gb_own = gram(b_ref[...])
    gb = gb_own
    for ref in blocks[1:]:
        gb = gb + gram(ref[h_own:])
    gc = gram(heights[...])
    ga = ga_ref[...]
    to_radius, to_height, to_source = scales
    pa_ref[...] = (times(a_ref[...], gb_own * gc) - pa) * to_radius
    ps_ref[...] = (times(b_ref[...], ga * gc) - ps) * to_source
    ph_ref[...] = times(blocks[0][0:h_own], ga * gb) * to_height


def local_any(slab, radius_factor, height_factor, source_factor, scales):
    n_src = lax.axis_size("src")
    r_rows, s_rows, width = slab.shape
    h_own, rank = height_factor.shape
    work = 2 * r_rows * s_rows * width * rank
    src_bits = [1 << i for i in range(n_src.bit_length() - 1)]
    a, b, cb, ga = call(
        prepare,
        [((r_rows, rank), BF16), ((s_rows, rank), BF16), ((h_own + s_rows, rank), BF16), ((rank, rank), F32)],
        (radius_factor, source_factor, height_factor),
        work // 2,
        resident=False,
    )
    blocks = {0: cb}
    for bit in reversed(src_bits):
        blocks[bit] = swap(cb, "src", bit)
    if h_own % LANES == 0:
        offsets = list(range(n_src))
        (g_away,) = call(
            functools.partial(height_terms, offsets[1::2]), [((width // 2, rank), F32)], (slab, a, b), work // 2
        )
        g_in = swap(g_away, "src", 1)
        ready = after(a, g_away, *[blocks[bit] for bit in src_bits])
        (g_keep,) = call(
            functools.partial(height_terms, offsets[0::2]), [((width // 2, rank), F32)], (slab, ready, b), work // 2
        )
    else:
        (g,) = call(functools.partial(height_terms, None), [((width, rank), F32)], (slab, a, b), work)
        me = lax.axis_index("src")
        g = jnp.take(g.reshape(n_src, h_own, rank), me ^ jnp.arange(n_src), axis=0)
        g_away, g_keep = (g[i::2].reshape(width // 2, rank) for i in (1, 0))
        g_in = swap(g_away, "src", 1)
    for o in range(1, n_src):
        if o not in blocks:
            low = o & -o
            blocks[o] = swap(after(blocks[o ^ low], g_away), "src", low)
    g = g_keep + g_in
    for bit in src_bits[1:-1]:
        g = g.reshape(-1, 2, h_own, rank)
        g = (g[:, 0] + swap(g[:, 1], "src", bit)).reshape(-1, rank)
    share_in = swap(g[h_own:], "src", src_bits[-1])
    pa, ps, ph = call(
        functools.partial(project, scales, n_src),
        [((r_rows, rank), F32), ((s_rows, rank), F32), ((h_own, rank), F32)],
        (slab, a, b, ga, *[blocks[o] for o in range(n_src)]),
        work,
        scratch=[pltpu.VMEM((width, rank), BF16)],
    )
    ph = ph - (g[:h_own] + share_in) * scales[1]
    e = exponent(jnp.maximum(column_top(ph), column_top(ps)))
    return pa, pack(jnp.concatenate([ph, ps, jnp.zeros((TAIL, rank), F32)], axis=0), e)


def finish(v_ref, pa_ref, in_ref, r_ref, h_ref, s_ref):
    h_own = h_ref.shape[0]
    r_ref[...] = pa_ref[...] + in_ref[...]
    h_ref[...] = v_ref[0:h_own]
    s_ref[...] = v_ref[h_own : h_own + s_ref.shape[0]]


def pack(v, e):
    rows = lax.broadcasted_iota(jnp.int32, v.shape, 0)
    return jnp.where(rows < v.shape[0] - TAIL, v * jnp.exp2(TOP - e), e).astype(F16)


def unpack(m):
    e = m[-1:].astype(F32)
    return m.astype(F32) * jnp.exp2(e - TOP), e


def per_device(slab, radius_factor, height_factor, source_factor):
    n_rad, n_src = lax.axis_size("rad"), lax.axis_size("src")
    r_rows, s_rows, width = slab.shape
    h_own, rank = height_factor.shape
    total_r, total_s = r_rows * n_rad, s_rows * n_src
    scales = (
        (total_s * width) ** -0.5,
        (total_r * total_s) ** -0.5,
        (total_r * width) ** -0.5,
    )
    src_bits = [1 << i for i in range(n_src.bit_length() - 1)]
    rad_bits = [1 << i for i in range(n_rad.bit_length() - 1)]

    local = local_four if n_src == 4 and h_own % LANES == 0 else local_any
    pa, m = local(slab, radius_factor, height_factor, source_factor, scales)
    bits = src_bits[::-1]
    stages = [rad_bits[i : i + 2] for i in range(0, len(rad_bits), 2)]
    for i, stage in enumerate(stages):
        others = stage if len(stage) == 1 else [*stage, sum(stage)]
        terms = [unpack(m)] + [unpack(swap(m, "rad", o)) for o in others]
        if len(bits) > 1:
            pa = after(pa, m)
            pa = pa + swap(pa, "src", bits.pop(0))
        values = [value for value, _ in terms]
        while len(values) > 1:
            values = [a + b for a, b in zip(values[0::2], values[1::2])]
        (v,) = values
        if i + 1 < len(stages):
            m = pack(v, functools.reduce(jnp.maximum, [x for _, x in terms]) + len(stage))
    while len(bits) > 1:
        pa = pa + swap(pa, "src", bits.pop(0))
    pa_in = swap(after(pa, m), "src", bits[0])
    return pl.pallas_call(
        finish,
        in_specs=[WHOLE] * 3,
        out_specs=[WHOLE] * 3,
        out_shape=[jax.ShapeDtypeStruct((rows, rank), F32) for rows in (r_rows, h_own, s_rows)],
    )(inside(v), inside(pa), inside(pa_in))


def solution(mesh):
    return jax.shard_map(
        per_device,
        mesh=mesh,
        in_specs=(P("rad", "src", None), P("rad", None), P("src", None), P("src", None)),
        out_specs=(P("rad", None), P("src", None), P("src", None)),
        check_vma=False,
    )
```

```python
import functools

import jax
import jax.numpy as jnp
from jax import lax
from jax.experimental import pallas as pl
from jax.experimental.pallas import tpu as pltpu
from jax.sharding import PartitionSpec as P

F32 = jnp.float32
BF16 = jnp.bfloat16
F16 = jnp.float16
VMEM_LIMIT = 32 * 1024 * 1024
LOAD_LIMIT = 54 * 1024 * 1024 + 512 * 1024
LANES = 128
CHUNKS = 8
TAIL = 8
TOP = 13.0
WHOLE = pl.BlockSpec(memory_space=pltpu.VMEM)


def inside(x):
    return pltpu.with_memory_space_constraint(x, pltpu.VMEM)


def after(x, *others):
    return lax.optimization_barrier((x, *others))[0]


def swap(x, axis, bit):
    return lax.ppermute(x, axis, [(i, i ^ bit) for i in range(lax.axis_size(axis))])


def call(body, outs, args, flops, resident=True, scratch=()):
    return pl.pallas_call(
        body,
        in_specs=[WHOLE] * len(args),
        out_specs=[WHOLE] * len(outs),
        out_shape=[pltpu.VMEM(shape, dtype) for shape, dtype in outs],
        scratch_shapes=scratch,
        compiler_params=pltpu.CompilerParams(vmem_limit_bytes=VMEM_LIMIT),
        cost_estimate=pl.CostEstimate(flops=flops, bytes_accessed=0, transcendentals=0),
    )(*[inside(a) if resident else a for a in args])


def gram(x):
    return lax.dot_general(x, x, (((0,), (0,)), ((), ())), preferred_element_type=F32)


def halves(m):
    hi = m.astype(BF16)
    return hi, (m - hi.astype(F32)).astype(BF16)


def times(x, m):
    hi, lo = halves(m)
    return jnp.dot(x, hi, preferred_element_type=F32) + jnp.dot(x, lo, preferred_element_type=F32)


def exponent(top):
    return jnp.clip(jnp.ceil(jnp.log2(jnp.maximum(top, 1e-30))), -100.0, 100.0)


def column_top(v):
    return jnp.max(jnp.abs(v), axis=0, keepdims=True)


def prepare(a_ref, b_ref, c_ref, a_out, b_out, cb_out, ga_out):
    h_own = c_ref.shape[0]
    cb_out[0:h_own] = c_ref[...]
    cb_out[h_own:] = b_ref[...]
    a_out[...] = a_ref[...]
    b_out[...] = b_ref[...]
    ga_out[...] = gram(a_ref[...])


def height_terms(offsets, x_ref, a_ref, b_ref, g_ref):
    s_rows, rank = b_ref.shape
    r_rows = a_ref.shape[0]
    rows = r_rows * s_rows
    kr = (a_ref[...][:, None, :] * b_ref[...][None]).reshape(rows, rank)
    if offsets is None:
        x = x_ref[...]
    else:
        width = g_ref.shape[0] // len(offsets)
        me = lax.axis_index("src")
        x = jnp.concatenate(
            [x_ref[:, :, pl.ds(pl.multiple_of((me ^ o) * width, width), width)] for o in offsets], axis=2
        )
    g_ref[...] = lax.dot_general(
        x.reshape(rows, x.shape[2]), kr, (((0,), (0,)), ((), ())), preferred_element_type=F32
    )


def load(offsets, x_hbm, a_hbm, b_hbm, c_hbm, x_ref, a_ref, b_ref, cb_ref, ga_ref, g_ref, sems):
    s_rows, rank = b_ref.shape
    r_rows = a_ref.shape[0]
    h_own = c_hbm.shape[0]
    width = g_ref.shape[0] // len(offsets)
    small = [
        pltpu.make_async_copy(a_hbm, a_ref, sems.at[0]),
        pltpu.make_async_copy(b_hbm, b_ref, sems.at[1]),
        pltpu.make_async_copy(c_hbm, cb_ref.at[pl.ds(0, h_own)], sems.at[2]),
        pltpu.make_async_copy(b_hbm, cb_ref.at[pl.ds(h_own, s_rows)], sems.at[3]),
    ]
    rows = r_rows // CHUNKS
    chunks = [
        pltpu.make_async_copy(x_hbm.at[pl.ds(i * rows, rows)], x_ref.at[pl.ds(i * rows, rows)], sems.at[4 + i])
        for i in range(CHUNKS)
    ]
    for copy in small + chunks:
        copy.start()
    for copy in small:
        copy.wait()
    ga_ref[...] = gram(a_ref[...])
    me = lax.axis_index("src")
    at = [pl.ds(pl.multiple_of((me ^ o) * width, width), width) for o in offsets]
    for i, copy in enumerate(chunks):
        mine = pl.ds(i * rows, rows)
        kr = (a_ref[mine][:, None, :] * b_ref[...][None]).reshape(rows * s_rows, rank)
        copy.wait()
        x = jnp.concatenate([x_ref[mine, :, a] for a in at], axis=2).reshape(rows * s_rows, 2 * width)
        part = lax.dot_general(x, kr, (((0,), (0,)), ((), ())), preferred_element_type=F32)
        g_ref[...] = part if i == 0 else g_ref[...] + part


def begin(o_ref):
    o_ref[...] = jnp.zeros_like(o_ref)


def products(a_in, b_in, t_ref, a_ref, b_ref, ga_ref):
    a_ref[...] = a_in[...]
    b_ref[...] = b_in[...]
    ga_ref[...] = gram(a_in[...])


def terms(b_ref, b1_ref, ga_ref, own_ref, c2_ref, keep_ref, away_ref):
    parts = halves(ga_ref[...] * (gram(b_ref[...]) + gram(b1_ref[...])))
    for rows, out in ((own_ref, keep_ref), (c2_ref, away_ref)):
        out[...] = sum(jnp.dot(rows[...], part, preferred_element_type=F32) for part in parts)


def write_message(m_ref, *parts):
    top = functools.reduce(jnp.maximum, [column_top(part) for part in parts])
    e = exponent(top)
    scale = jnp.exp2(TOP - e)
    at = 0
    for part in parts:
        m_ref[at : at + part.shape[0]] = part * scale
        at += part.shape[0]
    m_ref[at:] = jnp.broadcast_to(e, (m_ref.shape[0] - at, e.shape[1]))


def meet(to_height, g_ref, in_ref, keep_in, away_in, keep_ref, m_ref):
    h_own = keep_in.shape[0]
    g = g_ref[...] + in_ref[...]
    keep_ref[...] = (keep_in[...] - g[0:h_own]) * to_height
    write_message(m_ref, (away_in[...] - g[h_own:]) * to_height)


def combine(keep_ref, in_ref, ps_ref, m_ref):
    h_own = keep_ref.shape[0]
    share = keep_ref[...] + in_ref[0:h_own] * jnp.exp2(in_ref[h_own : h_own + 1] - TOP)
    write_message(m_ref, share, ps_ref[...])


def radius(to_radius, a_ref, b_ref, gc_ref, slab_ref, pa_ref):
    pa_ref[...] = (times(a_ref[...], gram(b_ref[...]) * gc_ref[...]) - slab_ref[...]) * to_radius


def project_four(to_source, x_ref, a_ref, b_ref, ga_ref, c0, c1, c2, c3, pa_ref, ps_ref, gc_ref, heights):
    s_rows, rank = b_ref.shape
    r_rows = a_ref.shape[0]
    h_own = c0.shape[0]
    me = lax.axis_index("src")
    for o, part in enumerate((c0, c1, c2, c3)):
        heights[pl.ds(pl.multiple_of((me ^ o) * h_own, h_own), h_own)] = part[...]
    x = x_ref[...].reshape(r_rows * s_rows, x_ref.shape[2])
    proj = jnp.dot(x, heights[...], preferred_element_type=F32).reshape(r_rows, s_rows, rank)
    pa_ref[...] = (proj * b_ref[...].astype(F32)[None]).sum(1)
    ps = (proj * a_ref[...].astype(F32)[:, None, :]).sum(0)
    gc = gram(heights[...])
    gc_ref[...] = gc
    ps_ref[...] = (times(b_ref[...], ga_ref[...] * gc) - ps) * to_source


def local_four(slab, radius_factor, height_factor, source_factor, scales):
    r_rows, s_rows, width = slab.shape
    h_own, rank = height_factor.shape
    work = 2 * r_rows * s_rows * width * rank
    c2 = swap(height_factor, "src", 2)
    c3 = swap(height_factor, "src", 3)
    c1 = swap(height_factor, "src", 1)
    b1 = swap(source_factor, "src", 1)
    (tick,) = call(begin, [((8, LANES), F32)], (), 2 * work)
    a, b, ga = call(
        products,
        [((r_rows, rank), BF16), ((s_rows, rank), BF16), ((rank, rank), F32)],
        (radius_factor, source_factor, tick),
        work // 8,
        resident=False,
    )
    half, block = [((width // 2, rank), F32)], [((h_own, rank), F32)]
    (g_away,) = call(functools.partial(height_terms, (1, 3)), half, (slab, a, b), 2 * work, resident=False)
    g_in = swap(g_away, "src", 1)
    (g_keep,) = call(
        functools.partial(height_terms, (0, 2)), half, (slab, after(a, g_away, b1), b), 4 * work
    )
    keep, away = call(terms, block * 2, (after(b, g_keep), b1, ga, height_factor, c2), work // 8)
    keep, away = call(
        functools.partial(meet, scales[1]),
        block + [((h_own + TAIL, rank), F32)],
        (g_keep, g_in, keep, away),
        work // 32,
    )
    away = away.astype(F16)
    share_in = swap(away, "src", 2)
    pa, ps, gc = call(
        functools.partial(project_four, scales[2]),
        [((r_rows, rank), F32), ((s_rows, rank), F32), ((rank, rank), F32)],
        (slab, after(a, away), b, ga, height_factor, c1, c2, c3),
        work,
        scratch=[pltpu.VMEM((width, rank), BF16)],
    )
    (m,) = call(combine, [((h_own + s_rows + TAIL, rank), F32)], (keep, share_in.astype(F32), ps), work // 32)
    m = m.astype(F16)
    (pa,) = call(
        functools.partial(radius, scales[0]), [((r_rows, rank), F32)], (a, b, gc, after(pa, m)), work // 32
    )
    return pa, m


def project(scales, n_src, x_ref, a_ref, b_ref, ga_ref, *refs):
    blocks, (pa_ref, ps_ref, ph_ref, heights) = refs[:n_src], refs[n_src:]
    s_rows, rank = b_ref.shape
    r_rows = a_ref.shape[0]
    h_own = blocks[0].shape[0] - s_rows
    me = lax.axis_index("src")
    for o, ref in enumerate(blocks):
        heights[pl.ds(pl.multiple_of((me ^ o) * h_own, h_own), h_own)] = ref[0:h_own]
    x = x_ref[...].reshape(r_rows * s_rows, x_ref.shape[2])
    proj = jnp.dot(x, heights[...], preferred_element_type=F32).reshape(r_rows, s_rows, rank)
    pa = (proj * b_ref[...].astype(F32)[None]).sum(1)
    ps = (proj * a_ref[...].astype(F32)[:, None, :]).sum(0)
    gb_own = gram(b_ref[...])
    gb = gb_own
    for ref in blocks[1:]:
        gb = gb + gram(ref[h_own:])
    gc = gram(heights[...])
    ga = ga_ref[...]
    to_radius, to_height, to_source = scales
    pa_ref[...] = (times(a_ref[...], gb_own * gc) - pa) * to_radius
    ps_ref[...] = (times(b_ref[...], ga * gc) - ps) * to_source
    ph_ref[...] = times(blocks[0][0:h_own], ga * gb) * to_height


def local_any(slab, radius_factor, height_factor, source_factor, scales):
    n_src = lax.axis_size("src")
    r_rows, s_rows, width = slab.shape
    h_own, rank = height_factor.shape
    work = 2 * r_rows * s_rows * width * rank
    src_bits = [1 << i for i in range(n_src.bit_length() - 1)]
    a, b, cb, ga = call(
        prepare,
        [((r_rows, rank), BF16), ((s_rows, rank), BF16), ((h_own + s_rows, rank), BF16), ((rank, rank), F32)],
        (radius_factor, source_factor, height_factor),
        work // 2,
        resident=False,
    )
    blocks = {0: cb}
    for bit in reversed(src_bits):
        blocks[bit] = swap(cb, "src", bit)
    if h_own % LANES == 0:
        offsets = list(range(n_src))
        (g_away,) = call(
            functools.partial(height_terms, offsets[1::2]), [((width // 2, rank), F32)], (slab, a, b), work // 2
        )
        g_in = swap(g_away, "src", 1)
        ready = after(a, g_away, *[blocks[bit] for bit in src_bits])
        (g_keep,) = call(
            functools.partial(height_terms, offsets[0::2]), [((width // 2, rank), F32)], (slab, ready, b), work // 2
        )
    else:
        (g,) = call(functools.partial(height_terms, None), [((width, rank), F32)], (slab, a, b), work)
        me = lax.axis_index("src")
        g = jnp.take(g.reshape(n_src, h_own, rank), me ^ jnp.arange(n_src), axis=0)
        g_away, g_keep = (g[i::2].reshape(width // 2, rank) for i in (1, 0))
        g_in = swap(g_away, "src", 1)
    for o in range(1, n_src):
        if o not in blocks:
            low = o & -o
            blocks[o] = swap(after(blocks[o ^ low], g_away), "src", low)
    g = g_keep + g_in
    for bit in src_bits[1:-1]:
        g = g.reshape(-1, 2, h_own, rank)
        g = (g[:, 0] + swap(g[:, 1], "src", bit)).reshape(-1, rank)
    share_in = swap(g[h_own:], "src", src_bits[-1])
    pa, ps, ph = call(
        functools.partial(project, scales, n_src),
        [((r_rows, rank), F32), ((s_rows, rank), F32), ((h_own, rank), F32)],
        (slab, a, b, ga, *[blocks[o] for o in range(n_src)]),
        work,
        scratch=[pltpu.VMEM((width, rank), BF16)],
    )
    ph = ph - (g[:h_own] + share_in) * scales[1]
    e = exponent(jnp.maximum(column_top(ph), column_top(ps)))
    return pa, pack(jnp.concatenate([ph, ps, jnp.zeros((TAIL, rank), F32)], axis=0), e)


def finish(v_ref, pa_ref, in_ref, r_ref, h_ref, s_ref):
    h_own = h_ref.shape[0]
    r_ref[...] = pa_ref[...] + in_ref[...]
    h_ref[...] = v_ref[0:h_own]
    s_ref[...] = v_ref[h_own : h_own + s_ref.shape[0]]


def pack(v, e):
    rows = lax.broadcasted_iota(jnp.int32, v.shape, 0)
    return jnp.where(rows < v.shape[0] - TAIL, v * jnp.exp2(TOP - e), e).astype(F16)


def unpack(m):
    e = m[-1:].astype(F32)
    return m.astype(F32) * jnp.exp2(e - TOP), e


def per_device(slab, radius_factor, height_factor, source_factor):
    n_rad, n_src = lax.axis_size("rad"), lax.axis_size("src")
    r_rows, s_rows, width = slab.shape
    h_own, rank = height_factor.shape
    total_r, total_s = r_rows * n_rad, s_rows * n_src
    scales = (
        (total_s * width) ** -0.5,
        (total_r * total_s) ** -0.5,
        (total_r * width) ** -0.5,
    )
    src_bits = [1 << i for i in range(n_src.bit_length() - 1)]
    rad_bits = [1 << i for i in range(n_rad.bit_length() - 1)]

    local = local_four if n_src == 4 and h_own % LANES == 0 else local_any
    pa, m = local(slab, radius_factor, height_factor, source_factor, scales)
    bits = src_bits[::-1]
    stages = [rad_bits[i : i + 2] for i in range(0, len(rad_bits), 2)]
    for i, stage in enumerate(stages):
        others = stage if len(stage) == 1 else [*stage, sum(stage)]
        terms = [unpack(m)] + [unpack(swap(m, "rad", o)) for o in others]
        if len(bits) > 1:
            pa = after(pa, m)
            pa = pa + swap(pa, "src", bits.pop(0))
        values = [value for value, _ in terms]
        while len(values) > 1:
            values = [a + b for a, b in zip(values[0::2], values[1::2])]
        (v,) = values
        if i + 1 < len(stages):
            m = pack(v, functools.reduce(jnp.maximum, [x for _, x in terms]) + len(stage))
    while len(bits) > 1:
        pa = pa + swap(pa, "src", bits.pop(0))
    pa_in = swap(after(pa, m), "src", bits[0])
    return pl.pallas_call(
        finish,
        in_specs=[WHOLE] * 3,
        out_specs=[WHOLE] * 3,
        out_shape=[jax.ShapeDtypeStruct((rows, rank), F32) for rows in (r_rows, h_own, s_rows)],
    )(inside(v), inside(pa), inside(pa_in))


def solution(mesh):
    return jax.shard_map(
        per_device,
        mesh=mesh,
        in_specs=(P("rad", "src", None), P("rad", None), P("src", None), P("src", None)),
        out_specs=(P("rad", None), P("src", None), P("src", None)),
        check_vma=False,
    )
```

```python
import functools

import jax
import jax.numpy as jnp
from jax import lax
from jax.experimental import pallas as pl
from jax.experimental.pallas import tpu as pltpu
from jax.sharding import PartitionSpec as P

F32 = jnp.float32
BF16 = jnp.bfloat16
F16 = jnp.float16
VMEM_LIMIT = 32 * 1024 * 1024
LOAD_LIMIT = 54 * 1024 * 1024 + 512 * 1024
LANES = 128
CHUNKS = 8
TAIL = 8
TOP = 13.0
WHOLE = pl.BlockSpec(memory_space=pltpu.VMEM)


def inside(x):
    return pltpu.with_memory_space_constraint(x, pltpu.VMEM)


def after(x, *others):
    return lax.optimization_barrier((x, *others))[0]


def swap(x, axis, bit):
    return lax.ppermute(x, axis, [(i, i ^ bit) for i in range(lax.axis_size(axis))])


def call(body, outs, args, flops, resident=True, scratch=()):
    return pl.pallas_call(
        body,
        in_specs=[WHOLE] * len(args),
        out_specs=[WHOLE] * len(outs),
        out_shape=[pltpu.VMEM(shape, dtype) for shape, dtype in outs],
        scratch_shapes=scratch,
        compiler_params=pltpu.CompilerParams(vmem_limit_bytes=VMEM_LIMIT),
        cost_estimate=pl.CostEstimate(flops=flops, bytes_accessed=0, transcendentals=0),
    )(*[inside(a) if resident else a for a in args])


def gram(x):
    return lax.dot_general(x, x, (((0,), (0,)), ((), ())), preferred_element_type=F32)


def halves(m):
    hi = m.astype(BF16)
    return hi, (m - hi.astype(F32)).astype(BF16)


def times(x, m):
    hi, lo = halves(m)
    return jnp.dot(x, hi, preferred_element_type=F32) + jnp.dot(x, lo, preferred_element_type=F32)


def exponent(top):
    return jnp.clip(jnp.ceil(jnp.log2(jnp.maximum(top, 1e-30))), -100.0, 100.0)


def column_top(v):
    return jnp.max(jnp.abs(v), axis=0, keepdims=True)


def prepare(a_ref, b_ref, c_ref, a_out, b_out, cb_out, ga_out):
    h_own = c_ref.shape[0]
    cb_out[0:h_own] = c_ref[...]
    cb_out[h_own:] = b_ref[...]
    a_out[...] = a_ref[...]
    b_out[...] = b_ref[...]
    ga_out[...] = gram(a_ref[...])


def height_terms(offsets, x_ref, a_ref, b_ref, g_ref):
    s_rows, rank = b_ref.shape
    r_rows = a_ref.shape[0]
    rows = r_rows * s_rows
    kr = (a_ref[...][:, None, :] * b_ref[...][None]).reshape(rows, rank)
    if offsets is None:
        x = x_ref[...]
    else:
        width = g_ref.shape[0] // len(offsets)
        me = lax.axis_index("src")
        x = jnp.concatenate(
            [x_ref[:, :, pl.ds(pl.multiple_of((me ^ o) * width, width), width)] for o in offsets], axis=2
        )
    g_ref[...] = lax.dot_general(
        x.reshape(rows, x.shape[2]), kr, (((0,), (0,)), ((), ())), preferred_element_type=F32
    )


def load(offsets, x_hbm, a_hbm, b_hbm, c_hbm, x_ref, a_ref, b_ref, cb_ref, ga_ref, g_ref, sems):
    s_rows, rank = b_ref.shape
    r_rows = a_ref.shape[0]
    h_own = c_hbm.shape[0]
    width = g_ref.shape[0] // len(offsets)
    small = [
        pltpu.make_async_copy(a_hbm, a_ref, sems.at[0]),
        pltpu.make_async_copy(b_hbm, b_ref, sems.at[1]),
        pltpu.make_async_copy(c_hbm, cb_ref.at[pl.ds(0, h_own)], sems.at[2]),
        pltpu.make_async_copy(b_hbm, cb_ref.at[pl.ds(h_own, s_rows)], sems.at[3]),
    ]
    rows = r_rows // CHUNKS
    chunks = [
        pltpu.make_async_copy(x_hbm.at[pl.ds(i * rows, rows)], x_ref.at[pl.ds(i * rows, rows)], sems.at[4 + i])
        for i in range(CHUNKS)
    ]
    for copy in small + chunks:
        copy.start()
    for copy in small:
        copy.wait()
    ga_ref[...] = gram(a_ref[...])
    me = lax.axis_index("src")
    at = [pl.ds(pl.multiple_of((me ^ o) * width, width), width) for o in offsets]
    for i, copy in enumerate(chunks):
        mine = pl.ds(i * rows, rows)
        kr = (a_ref[mine][:, None, :] * b_ref[...][None]).reshape(rows * s_rows, rank)
        copy.wait()
        x = jnp.concatenate([x_ref[mine, :, a] for a in at], axis=2).reshape(rows * s_rows, 2 * width)
        part = lax.dot_general(x, kr, (((0,), (0,)), ((), ())), preferred_element_type=F32)
        g_ref[...] = part if i == 0 else g_ref[...] + part


def begin(o_ref):
    o_ref[...] = jnp.zeros_like(o_ref)


def products(a_in, b_in, t_ref, a_ref, b_ref, ga_ref):
    a_ref[...] = a_in[...]
    b_ref[...] = b_in[...]
    ga_ref[...] = gram(a_in[...])


def terms(b_ref, b1_ref, ga_ref, own_ref, c2_ref, keep_ref, away_ref):
    parts = halves(ga_ref[...] * (gram(b_ref[...]) + gram(b1_ref[...])))
    for rows, out in ((own_ref, keep_ref), (c2_ref, away_ref)):
        out[...] = sum(jnp.dot(rows[...], part, preferred_element_type=F32) for part in parts)


def write_message(m_ref, *parts):
    top = functools.reduce(jnp.maximum, [column_top(part) for part in parts])
    e = exponent(top)
    scale = jnp.exp2(TOP - e)
    at = 0
    for part in parts:
        m_ref[at : at + part.shape[0]] = part * scale
        at += part.shape[0]
    m_ref[at:] = jnp.broadcast_to(e, (m_ref.shape[0] - at, e.shape[1]))


def meet(to_height, g_ref, in_ref, keep_in, away_in, keep_ref, m_ref):
    h_own = keep_in.shape[0]
    g = g_ref[...] + in_ref[...]
    keep_ref[...] = (keep_in[...] - g[0:h_own]) * to_height
    write_message(m_ref, (away_in[...] - g[h_own:]) * to_height)


def combine(keep_ref, in_ref, ps_ref, m_ref):
    h_own = keep_ref.shape[0]
    share = keep_ref[...] + in_ref[0:h_own] * jnp.exp2(in_ref[h_own : h_own + 1] - TOP)
    write_message(m_ref, share, ps_ref[...])


def radius(to_radius, a_ref, b_ref, gc_ref, slab_ref, pa_ref):
    pa_ref[...] = (times(a_ref[...], gram(b_ref[...]) * gc_ref[...]) - slab_ref[...]) * to_radius


def project_four(to_source, x_ref, a_ref, b_ref, ga_ref, c0, c1, c2, c3, pa_ref, ps_ref, gc_ref, heights):
    s_rows, rank = b_ref.shape
    r_rows = a_ref.shape[0]
    h_own = c0.shape[0]
    me = lax.axis_index("src")
    for o, part in enumerate((c0, c1, c2, c3)):
        heights[pl.ds(pl.multiple_of((me ^ o) * h_own, h_own), h_own)] = part[...]
    x = x_ref[...].reshape(r_rows * s_rows, x_ref.shape[2])
    proj = jnp.dot(x, heights[...], preferred_element_type=F32).reshape(r_rows, s_rows, rank)
    pa_ref[...] = (proj * b_ref[...].astype(F32)[None]).sum(1)
    ps = (proj * a_ref[...].astype(F32)[:, None, :]).sum(0)
    gc = gram(heights[...])
    gc_ref[...] = gc
    ps_ref[...] = (times(b_ref[...], ga_ref[...] * gc) - ps) * to_source


def local_four(slab, radius_factor, height_factor, source_factor, scales):
    r_rows, s_rows, width = slab.shape
    h_own, rank = height_factor.shape
    work = 2 * r_rows * s_rows * width * rank
    c2 = swap(height_factor, "src", 2)
    c3 = swap(height_factor, "src", 3)
    c1 = swap(height_factor, "src", 1)
    b1 = swap(source_factor, "src", 1)
    (tick,) = call(begin, [((8, LANES), F32)], (), 2 * work)
    a, b, ga = call(
        products,
        [((r_rows, rank), BF16), ((s_rows, rank), BF16), ((rank, rank), F32)],
        (radius_factor, source_factor, tick),
        work // 8,
        resident=False,
    )
    half, block = [((width // 2, rank), F32)], [((h_own, rank), F32)]
    (g_away,) = call(functools.partial(height_terms, (1, 3)), half, (slab, a, b), 2 * work, resident=False)
    g_in = swap(g_away, "src", 1)
    (g_keep,) = call(
        functools.partial(height_terms, (0, 2)), half, (slab, after(a, g_away, b1), b), 4 * work
    )
    keep, away = call(terms, block * 2, (after(b, g_keep), b1, ga, height_factor, c2), work // 8)
    keep, away = call(
        functools.partial(meet, scales[1]),
        block + [((h_own + TAIL, rank), F32)],
        (g_keep, g_in, keep, away),
        work // 32,
    )
    away = away.astype(F16)
    share_in = swap(away, "src", 2)
    pa, ps, gc = call(
        functools.partial(project_four, scales[2]),
        [((r_rows, rank), F32), ((s_rows, rank), F32), ((rank, rank), F32)],
        (slab, after(a, away), b, ga, height_factor, c1, c2, c3),
        work,
        scratch=[pltpu.VMEM((width, rank), BF16)],
    )
    (m,) = call(combine, [((h_own + s_rows + TAIL, rank), F32)], (keep, share_in.astype(F32), ps), work // 32)
    m = m.astype(F16)
    (pa,) = call(
        functools.partial(radius, scales[0]), [((r_rows, rank), F32)], (a, b, gc, after(pa, m)), work // 32
    )
    return pa, m


def project(scales, n_src, x_ref, a_ref, b_ref, ga_ref, *refs):
    blocks, (pa_ref, ps_ref, ph_ref, heights) = refs[:n_src], refs[n_src:]
    s_rows, rank = b_ref.shape
    r_rows = a_ref.shape[0]
    h_own = blocks[0].shape[0] - s_rows
    me = lax.axis_index("src")
    for o, ref in enumerate(blocks):
        heights[pl.ds(pl.multiple_of((me ^ o) * h_own, h_own), h_own)] = ref[0:h_own]
    x = x_ref[...].reshape(r_rows * s_rows, x_ref.shape[2])
    proj = jnp.dot(x, heights[...], preferred_element_type=F32).reshape(r_rows, s_rows, rank)
    pa = (proj * b_ref[...].astype(F32)[None]).sum(1)
    ps = (proj * a_ref[...].astype(F32)[:, None, :]).sum(0)
    gb_own = gram(b_ref[...])
    gb = gb_own
    for ref in blocks[1:]:
        gb = gb + gram(ref[h_own:])
    gc = gram(heights[...])
    ga = ga_ref[...]
    to_radius, to_height, to_source = scales
    pa_ref[...] = (times(a_ref[...], gb_own * gc) - pa) * to_radius
    ps_ref[...] = (times(b_ref[...], ga * gc) - ps) * to_source
    ph_ref[...] = times(blocks[0][0:h_own], ga * gb) * to_height


def local_any(slab, radius_factor, height_factor, source_factor, scales):
    n_src = lax.axis_size("src")
    r_rows, s_rows, width = slab.shape
    h_own, rank = height_factor.shape
    work = 2 * r_rows * s_rows * width * rank
    src_bits = [1 << i for i in range(n_src.bit_length() - 1)]
    a, b, cb, ga = call(
        prepare,
        [((r_rows, rank), BF16), ((s_rows, rank), BF16), ((h_own + s_rows, rank), BF16), ((rank, rank), F32)],
        (radius_factor, source_factor, height_factor),
        work // 2,
        resident=False,
    )
    blocks = {0: cb}
    for bit in reversed(src_bits):
        blocks[bit] = swap(cb, "src", bit)
    if h_own % LANES == 0:
        offsets = list(range(n_src))
        (g_away,) = call(
            functools.partial(height_terms, offsets[1::2]), [((width // 2, rank), F32)], (slab, a, b), work // 2
        )
        g_in = swap(g_away, "src", 1)
        ready = after(a, g_away, *[blocks[bit] for bit in src_bits])
        (g_keep,) = call(
            functools.partial(height_terms, offsets[0::2]), [((width // 2, rank), F32)], (slab, ready, b), work // 2
        )
    else:
        (g,) = call(functools.partial(height_terms, None), [((width, rank), F32)], (slab, a, b), work)
        me = lax.axis_index("src")
        g = jnp.take(g.reshape(n_src, h_own, rank), me ^ jnp.arange(n_src), axis=0)
        g_away, g_keep = (g[i::2].reshape(width // 2, rank) for i in (1, 0))
        g_in = swap(g_away, "src", 1)
    for o in range(1, n_src):
        if o not in blocks:
            low = o & -o
            blocks[o] = swap(after(blocks[o ^ low], g_away), "src", low)
    g = g_keep + g_in
    for bit in src_bits[1:-1]:
        g = g.reshape(-1, 2, h_own, rank)
        g = (g[:, 0] + swap(g[:, 1], "src", bit)).reshape(-1, rank)
    share_in = swap(g[h_own:], "src", src_bits[-1])
    pa, ps, ph = call(
        functools.partial(project, scales, n_src),
        [((r_rows, rank), F32), ((s_rows, rank), F32), ((h_own, rank), F32)],
        (slab, a, b, ga, *[blocks[o] for o in range(n_src)]),
        work,
        scratch=[pltpu.VMEM((width, rank), BF16)],
    )
    ph = ph - (g[:h_own] + share_in) * scales[1]
    e = exponent(jnp.maximum(column_top(ph), column_top(ps)))
    return pa, pack(jnp.concatenate([ph, ps, jnp.zeros((TAIL, rank), F32)], axis=0), e)


def finish(v_ref, pa_ref, in_ref, r_ref, h_ref, s_ref):
    h_own = h_ref.shape[0]
    r_ref[...] = pa_ref[...] + in_ref[...]
    h_ref[...] = v_ref[0:h_own]
    s_ref[...] = v_ref[h_own : h_own + s_ref.shape[0]]


def pack(v, e):
    rows = lax.broadcasted_iota(jnp.int32, v.shape, 0)
    return jnp.where(rows < v.shape[0] - TAIL, v * jnp.exp2(TOP - e), e).astype(F16)


def unpack(m):
    e = m[-1:].astype(F32)
    return m.astype(F32) * jnp.exp2(e - TOP), e


def per_device(slab, radius_factor, height_factor, source_factor):
    n_rad, n_src = lax.axis_size("rad"), lax.axis_size("src")
    r_rows, s_rows, width = slab.shape
    h_own, rank = height_factor.shape
    total_r, total_s = r_rows * n_rad, s_rows * n_src
    scales = (
        (total_s * width) ** -0.5,
        (total_r * total_s) ** -0.5,
        (total_r * width) ** -0.5,
    )
    src_bits = [1 << i for i in range(n_src.bit_length() - 1)]
    rad_bits = [1 << i for i in range(n_rad.bit_length() - 1)]

    local = local_four if n_src == 4 and h_own % LANES == 0 else local_any
    pa, m = local(slab, radius_factor, height_factor, source_factor, scales)
    bits = src_bits[::-1]
    stages = [rad_bits[i : i + 2] for i in range(0, len(rad_bits), 2)]
    for i, stage in enumerate(stages):
        others = stage if len(stage) == 1 else [sum(stage), stage[1], stage[0]]
        terms = [unpack(m)] + [unpack(swap(m, "rad", o)) for o in others]
        if len(bits) > 1:
            pa = after(pa, m)
            pa = pa + swap(pa, "src", bits.pop(0))
        values = [value for value, _ in terms]
        while len(values) > 1:
            values = [a + b for a, b in zip(values[0::2], values[1::2])]
        (v,) = values
        if i + 1 < len(stages):
            m = pack(v, functools.reduce(jnp.maximum, [x for _, x in terms]) + len(stage))
    while len(bits) > 1:
        pa = pa + swap(pa, "src", bits.pop(0))
    pa_in = swap(after(pa, m), "src", bits[0])
    return pl.pallas_call(
        finish,
        in_specs=[WHOLE] * 3,
        out_specs=[WHOLE] * 3,
        out_shape=[jax.ShapeDtypeStruct((rows, rank), F32) for rows in (r_rows, h_own, s_rows)],
    )(inside(v), inside(pa), inside(pa_in))


def solution(mesh):
    return jax.shard_map(
        per_device,
        mesh=mesh,
        in_specs=(P("rad", "src", None), P("rad", None), P("src", None), P("src", None)),
        out_specs=(P("rad", None), P("src", None), P("src", None)),
        check_vma=False,
    )
```

```python
import functools

import jax
import jax.numpy as jnp
from jax import lax
from jax.experimental import pallas as pl
from jax.experimental.pallas import tpu as pltpu
from jax.sharding import PartitionSpec as P

F32 = jnp.float32
BF16 = jnp.bfloat16
F16 = jnp.float16
VMEM_LIMIT = 32 * 1024 * 1024
LOAD_LIMIT = 54 * 1024 * 1024 + 512 * 1024
LANES = 128
CHUNKS = 8
TAIL = 8
TOP = 13.0
WHOLE = pl.BlockSpec(memory_space=pltpu.VMEM)


def inside(x):
    return pltpu.with_memory_space_constraint(x, pltpu.VMEM)


def after(x, *others):
    return lax.optimization_barrier((x, *others))[0]


def swap(x, axis, bit):
    return lax.ppermute(x, axis, [(i, i ^ bit) for i in range(lax.axis_size(axis))])


def call(body, outs, args, flops, resident=True, scratch=()):
    return pl.pallas_call(
        body,
        in_specs=[WHOLE] * len(args),
        out_specs=[WHOLE] * len(outs),
        out_shape=[pltpu.VMEM(shape, dtype) for shape, dtype in outs],
        scratch_shapes=scratch,
        compiler_params=pltpu.CompilerParams(vmem_limit_bytes=VMEM_LIMIT),
        cost_estimate=pl.CostEstimate(flops=flops, bytes_accessed=0, transcendentals=0),
    )(*[inside(a) if resident else a for a in args])


def gram(x):
    return lax.dot_general(x, x, (((0,), (0,)), ((), ())), preferred_element_type=F32)


def halves(m):
    hi = m.astype(BF16)
    return hi, (m - hi.astype(F32)).astype(BF16)


def times(x, m):
    hi, lo = halves(m)
    return jnp.dot(x, hi, preferred_element_type=F32) + jnp.dot(x, lo, preferred_element_type=F32)


def exponent(top):
    return jnp.clip(jnp.ceil(jnp.log2(jnp.maximum(top, 1e-30))), -100.0, 100.0)


def column_top(v):
    return jnp.max(jnp.abs(v), axis=0, keepdims=True)


def prepare(a_ref, b_ref, c_ref, a_out, b_out, cb_out, ga_out):
    h_own = c_ref.shape[0]
    cb_out[0:h_own] = c_ref[...]
    cb_out[h_own:] = b_ref[...]
    a_out[...] = a_ref[...]
    b_out[...] = b_ref[...]
    ga_out[...] = gram(a_ref[...])


def height_terms(offsets, x_ref, a_ref, b_ref, g_ref):
    s_rows, rank = b_ref.shape
    r_rows = a_ref.shape[0]
    rows = r_rows * s_rows
    kr = (a_ref[...][:, None, :] * b_ref[...][None]).reshape(rows, rank)
    if offsets is None:
        x = x_ref[...]
    else:
        width = g_ref.shape[0] // len(offsets)
        me = lax.axis_index("src")
        x = jnp.concatenate(
            [x_ref[:, :, pl.ds(pl.multiple_of((me ^ o) * width, width), width)] for o in offsets], axis=2
        )
    g_ref[...] = lax.dot_general(
        x.reshape(rows, x.shape[2]), kr, (((0,), (0,)), ((), ())), preferred_element_type=F32
    )


def load(offsets, x_hbm, a_hbm, b_hbm, c_hbm, x_ref, a_ref, b_ref, cb_ref, ga_ref, g_ref, sems):
    s_rows, rank = b_ref.shape
    r_rows = a_ref.shape[0]
    h_own = c_hbm.shape[0]
    width = g_ref.shape[0] // len(offsets)
    small = [
        pltpu.make_async_copy(a_hbm, a_ref, sems.at[0]),
        pltpu.make_async_copy(b_hbm, b_ref, sems.at[1]),
        pltpu.make_async_copy(c_hbm, cb_ref.at[pl.ds(0, h_own)], sems.at[2]),
        pltpu.make_async_copy(b_hbm, cb_ref.at[pl.ds(h_own, s_rows)], sems.at[3]),
    ]
    rows = r_rows // CHUNKS
    chunks = [
        pltpu.make_async_copy(x_hbm.at[pl.ds(i * rows, rows)], x_ref.at[pl.ds(i * rows, rows)], sems.at[4 + i])
        for i in range(CHUNKS)
    ]
    for copy in small + chunks:
        copy.start()
    for copy in small:
        copy.wait()
    ga_ref[...] = gram(a_ref[...])
    me = lax.axis_index("src")
    at = [pl.ds(pl.multiple_of((me ^ o) * width, width), width) for o in offsets]
    for i, copy in enumerate(chunks):
        mine = pl.ds(i * rows, rows)
        kr = (a_ref[mine][:, None, :] * b_ref[...][None]).reshape(rows * s_rows, rank)
        copy.wait()
        x = jnp.concatenate([x_ref[mine, :, a] for a in at], axis=2).reshape(rows * s_rows, 2 * width)
        part = lax.dot_general(x, kr, (((0,), (0,)), ((), ())), preferred_element_type=F32)
        g_ref[...] = part if i == 0 else g_ref[...] + part


def begin(o_ref):
    o_ref[...] = jnp.zeros_like(o_ref)


def products(a_in, b_in, t_ref, a_ref, b_ref, ga_ref):
    a_ref[...] = a_in[...]
    b_ref[...] = b_in[...]
    ga_ref[...] = gram(a_in[...])


def terms(b_ref, b1_ref, ga_ref, own_ref, c2_ref, keep_ref, away_ref):
    parts = halves(ga_ref[...] * (gram(b_ref[...]) + gram(b1_ref[...])))
    for rows, out in ((own_ref, keep_ref), (c2_ref, away_ref)):
        out[...] = sum(jnp.dot(rows[...], part, preferred_element_type=F32) for part in parts)


def write_message(m_ref, *parts):
    top = functools.reduce(jnp.maximum, [column_top(part) for part in parts])
    e = exponent(top)
    scale = jnp.exp2(TOP - e)
    at = 0
    for part in parts:
        m_ref[at : at + part.shape[0]] = part * scale
        at += part.shape[0]
    m_ref[at:] = jnp.broadcast_to(e, (m_ref.shape[0] - at, e.shape[1]))


def meet(to_height, g_ref, in_ref, keep_in, away_in, keep_ref, m_ref):
    h_own = keep_in.shape[0]
    g = g_ref[...] + in_ref[...]
    keep_ref[...] = (keep_in[...] - g[0:h_own]) * to_height
    write_message(m_ref, (away_in[...] - g[h_own:]) * to_height)


def combine(keep_ref, in_ref, ps_ref, m_ref):
    h_own = keep_ref.shape[0]
    share = keep_ref[...] + in_ref[0:h_own] * jnp.exp2(in_ref[h_own : h_own + 1] - TOP)
    write_message(m_ref, share, ps_ref[...])


def radius(to_radius, a_ref, b_ref, gc_ref, slab_ref, pa_ref):
    pa_ref[...] = (times(a_ref[...], gram(b_ref[...]) * gc_ref[...]) - slab_ref[...]) * to_radius


def project_four(to_source, x_ref, a_ref, b_ref, ga_ref, c0, c1, c2, c3, pa_ref, ps_ref, gc_ref, heights):
    s_rows, rank = b_ref.shape
    r_rows = a_ref.shape[0]
    h_own = c0.shape[0]
    me = lax.axis_index("src")
    for o, part in enumerate((c0, c1, c2, c3)):
        heights[pl.ds(pl.multiple_of((me ^ o) * h_own, h_own), h_own)] = part[...]
    x = x_ref[...].reshape(r_rows * s_rows, x_ref.shape[2])
    proj = jnp.dot(x, heights[...], preferred_element_type=F32).reshape(r_rows, s_rows, rank)
    pa_ref[...] = (proj * b_ref[...].astype(F32)[None]).sum(1)
    ps = (proj * a_ref[...].astype(F32)[:, None, :]).sum(0)
    gc = gram(heights[...])
    gc_ref[...] = gc
    ps_ref[...] = (times(b_ref[...], ga_ref[...] * gc) - ps) * to_source


def local_four(slab, radius_factor, height_factor, source_factor, scales):
    r_rows, s_rows, width = slab.shape
    h_own, rank = height_factor.shape
    work = 2 * r_rows * s_rows * width * rank
    c2 = swap(height_factor, "src", 2)
    c3 = swap(height_factor, "src", 3)
    c1 = swap(height_factor, "src", 1)
    b1 = swap(source_factor, "src", 1)
    (tick,) = call(begin, [((8, LANES), F32)], (), 2 * work)
    a, b, ga = call(
        products,
        [((r_rows, rank), BF16), ((s_rows, rank), BF16), ((rank, rank), F32)],
        (radius_factor, source_factor, tick),
        work // 8,
        resident=False,
    )
    half, block = [((width // 2, rank), F32)], [((h_own, rank), F32)]
    (g_away,) = call(functools.partial(height_terms, (1, 3)), half, (slab, a, b), 2 * work, resident=False)
    g_in = swap(g_away, "src", 1)
    (g_keep,) = call(
        functools.partial(height_terms, (0, 2)), half, (slab, after(a, g_away, b1), b), 4 * work
    )
    keep, away = call(terms, block * 2, (after(b, g_keep), b1, ga, height_factor, c2), work // 8)
    keep, away = call(
        functools.partial(meet, scales[1]),
        block + [((h_own + TAIL, rank), F32)],
        (g_keep, g_in, keep, away),
        work // 32,
    )
    away = away.astype(F16)
    share_in = swap(away, "src", 2)
    pa, ps, gc = call(
        functools.partial(project_four, scales[2]),
        [((r_rows, rank), F32), ((s_rows, rank), F32), ((rank, rank), F32)],
        (slab, after(a, away), b, ga, height_factor, c1, c2, c3),
        work,
        scratch=[pltpu.VMEM((width, rank), BF16)],
    )
    (m,) = call(combine, [((h_own + s_rows + TAIL, rank), F32)], (keep, share_in.astype(F32), ps), work // 32)
    m = m.astype(F16)
    (pa,) = call(
        functools.partial(radius, scales[0]), [((r_rows, rank), F32)], (a, b, gc, after(pa, m)), work // 32
    )
    return pa, m


def project(scales, n_src, x_ref, a_ref, b_ref, ga_ref, *refs):
    blocks, (pa_ref, ps_ref, ph_ref, heights) = refs[:n_src], refs[n_src:]
    s_rows, rank = b_ref.shape
    r_rows = a_ref.shape[0]
    h_own = blocks[0].shape[0] - s_rows
    me = lax.axis_index("src")
    for o, ref in enumerate(blocks):
        heights[pl.ds(pl.multiple_of((me ^ o) * h_own, h_own), h_own)] = ref[0:h_own]
    x = x_ref[...].reshape(r_rows * s_rows, x_ref.shape[2])
    proj = jnp.dot(x, heights[...], preferred_element_type=F32).reshape(r_rows, s_rows, rank)
    pa = (proj * b_ref[...].astype(F32)[None]).sum(1)
    ps = (proj * a_ref[...].astype(F32)[:, None, :]).sum(0)
    gb_own = gram(b_ref[...])
    gb = gb_own
    for ref in blocks[1:]:
        gb = gb + gram(ref[h_own:])
    gc = gram(heights[...])
    ga = ga_ref[...]
    to_radius, to_height, to_source = scales
    pa_ref[...] = (times(a_ref[...], gb_own * gc) - pa) * to_radius
    ps_ref[...] = (times(b_ref[...], ga * gc) - ps) * to_source
    ph_ref[...] = times(blocks[0][0:h_own], ga * gb) * to_height


def local_any(slab, radius_factor, height_factor, source_factor, scales):
    n_src = lax.axis_size("src")
    r_rows, s_rows, width = slab.shape
    h_own, rank = height_factor.shape
    work = 2 * r_rows * s_rows * width * rank
    src_bits = [1 << i for i in range(n_src.bit_length() - 1)]
    a, b, cb, ga = call(
        prepare,
        [((r_rows, rank), BF16), ((s_rows, rank), BF16), ((h_own + s_rows, rank), BF16), ((rank, rank), F32)],
        (radius_factor, source_factor, height_factor),
        work // 2,
        resident=False,
    )
    blocks = {0: cb}
    for bit in reversed(src_bits):
        blocks[bit] = swap(cb, "src", bit)
    if h_own % LANES == 0:
        offsets = list(range(n_src))
        (g_away,) = call(
            functools.partial(height_terms, offsets[1::2]), [((width // 2, rank), F32)], (slab, a, b), work // 2
        )
        g_in = swap(g_away, "src", 1)
        ready = after(a, g_away, *[blocks[bit] for bit in src_bits])
        (g_keep,) = call(
            functools.partial(height_terms, offsets[0::2]), [((width // 2, rank), F32)], (slab, ready, b), work // 2
        )
    else:
        (g,) = call(functools.partial(height_terms, None), [((width, rank), F32)], (slab, a, b), work)
        me = lax.axis_index("src")
        g = jnp.take(g.reshape(n_src, h_own, rank), me ^ jnp.arange(n_src), axis=0)
        g_away, g_keep = (g[i::2].reshape(width // 2, rank) for i in (1, 0))
        g_in = swap(g_away, "src", 1)
    for o in range(1, n_src):
        if o not in blocks:
            low = o & -o
            blocks[o] = swap(after(blocks[o ^ low], g_away), "src", low)
    g = g_keep + g_in
    for bit in src_bits[1:-1]:
        g = g.reshape(-1, 2, h_own, rank)
        g = (g[:, 0] + swap(g[:, 1], "src", bit)).reshape(-1, rank)
    share_in = swap(g[h_own:], "src", src_bits[-1])
    pa, ps, ph = call(
        functools.partial(project, scales, n_src),
        [((r_rows, rank), F32), ((s_rows, rank), F32), ((h_own, rank), F32)],
        (slab, a, b, ga, *[blocks[o] for o in range(n_src)]),
        work,
        scratch=[pltpu.VMEM((width, rank), BF16)],
    )
    ph = ph - (g[:h_own] + share_in) * scales[1]
    e = exponent(jnp.maximum(column_top(ph), column_top(ps)))
    return pa, pack(jnp.concatenate([ph, ps, jnp.zeros((TAIL, rank), F32)], axis=0), e)


def finish(v_ref, pa_ref, in_ref, r_ref, h_ref, s_ref):
    h_own = h_ref.shape[0]
    r_ref[...] = pa_ref[...] + in_ref[...]
    h_ref[...] = v_ref[0:h_own]
    s_ref[...] = v_ref[h_own : h_own + s_ref.shape[0]]


def pack(v, e):
    rows = lax.broadcasted_iota(jnp.int32, v.shape, 0)
    return jnp.where(rows < v.shape[0] - TAIL, v * jnp.exp2(TOP - e), e).astype(F16)


def unpack(m):
    e = m[-1:].astype(F32)
    return m.astype(F32) * jnp.exp2(e - TOP), e


def per_device(slab, radius_factor, height_factor, source_factor):
    n_rad, n_src = lax.axis_size("rad"), lax.axis_size("src")
    r_rows, s_rows, width = slab.shape
    h_own, rank = height_factor.shape
    total_r, total_s = r_rows * n_rad, s_rows * n_src
    scales = (
        (total_s * width) ** -0.5,
        (total_r * total_s) ** -0.5,
        (total_r * width) ** -0.5,
    )
    src_bits = [1 << i for i in range(n_src.bit_length() - 1)]
    rad_bits = [1 << i for i in range(n_rad.bit_length() - 1)]

    local = local_four if n_src == 4 and h_own % LANES == 0 else local_any
    pa, m = local(slab, radius_factor, height_factor, source_factor, scales)
    bits = src_bits[::-1]
    stages = [rad_bits[i : i + 2] for i in range(0, len(rad_bits), 2)]
    for i, stage in enumerate(stages):
        if len(stage) == 2:
            others = [sum(stage), stage[1], stage[0]]
        else:
            others = [stage[0] + (stage[0] // 2 if i else 0)]
        terms = [unpack(m)] + [unpack(swap(m, "rad", o)) for o in others]
        if len(bits) > 1:
            pa = after(pa, m)
            pa = pa + swap(pa, "src", bits.pop(0))
        values = [value for value, _ in terms]
        while len(values) > 1:
            values = [a + b for a, b in zip(values[0::2], values[1::2])]
        (v,) = values
        if i + 1 < len(stages):
            m = pack(v, functools.reduce(jnp.maximum, [x for _, x in terms]) + len(stage))
    while len(bits) > 1:
        pa = pa + swap(pa, "src", bits.pop(0))
    pa_in = swap(after(pa, m), "src", bits[0])
    return pl.pallas_call(
        finish,
        in_specs=[WHOLE] * 3,
        out_specs=[WHOLE] * 3,
        out_shape=[jax.ShapeDtypeStruct((rows, rank), F32) for rows in (r_rows, h_own, s_rows)],
    )(inside(v), inside(pa), inside(pa_in))


def solution(mesh):
    return jax.shard_map(
        per_device,
        mesh=mesh,
        in_specs=(P("rad", "src", None), P("rad", None), P("src", None), P("src", None)),
        out_specs=(P("rad", None), P("src", None), P("src", None)),
        check_vma=False,
    )
```

```python
import functools

import jax
import jax.numpy as jnp
from jax import lax
from jax.experimental import pallas as pl
from jax.experimental.pallas import tpu as pltpu
from jax.sharding import PartitionSpec as P

F32 = jnp.float32
BF16 = jnp.bfloat16
F16 = jnp.float16
VMEM_LIMIT = 32 * 1024 * 1024
LOAD_LIMIT = 54 * 1024 * 1024 + 512 * 1024
LANES = 128
CHUNKS = 8
TAIL = 8
TOP = 13.0
WHOLE = pl.BlockSpec(memory_space=pltpu.VMEM)


def inside(x):
    return pltpu.with_memory_space_constraint(x, pltpu.VMEM)


def after(x, *others):
    return lax.optimization_barrier((x, *others))[0]


def swap(x, axis, bit):
    return lax.ppermute(x, axis, [(i, i ^ bit) for i in range(lax.axis_size(axis))])


def call(body, outs, args, flops, resident=True, scratch=()):
    return pl.pallas_call(
        body,
        in_specs=[WHOLE] * len(args),
        out_specs=[WHOLE] * len(outs),
        out_shape=[pltpu.VMEM(shape, dtype) for shape, dtype in outs],
        scratch_shapes=scratch,
        compiler_params=pltpu.CompilerParams(vmem_limit_bytes=VMEM_LIMIT),
        cost_estimate=pl.CostEstimate(flops=flops, bytes_accessed=0, transcendentals=0),
    )(*[inside(a) if resident else a for a in args])


def gram(x):
    return lax.dot_general(x, x, (((0,), (0,)), ((), ())), preferred_element_type=F32)


def halves(m):
    hi = m.astype(BF16)
    return hi, (m - hi.astype(F32)).astype(BF16)


def times(x, m):
    hi, lo = halves(m)
    return jnp.dot(x, hi, preferred_element_type=F32) + jnp.dot(x, lo, preferred_element_type=F32)


def exponent(top):
    return jnp.clip(jnp.ceil(jnp.log2(jnp.maximum(top, 1e-30))), -100.0, 100.0)


def column_top(v):
    return jnp.max(jnp.abs(v), axis=0, keepdims=True)


def prepare(a_ref, b_ref, c_ref, a_out, b_out, cb_out, ga_out):
    h_own = c_ref.shape[0]
    cb_out[0:h_own] = c_ref[...]
    cb_out[h_own:] = b_ref[...]
    a_out[...] = a_ref[...]
    b_out[...] = b_ref[...]
    ga_out[...] = gram(a_ref[...])


def height_terms(offsets, x_ref, a_ref, b_ref, g_ref):
    s_rows, rank = b_ref.shape
    r_rows = a_ref.shape[0]
    rows = r_rows * s_rows
    kr = (a_ref[...][:, None, :] * b_ref[...][None]).reshape(rows, rank)
    if offsets is None:
        x = x_ref[...]
    else:
        width = g_ref.shape[0] // len(offsets)
        me = lax.axis_index("src")
        x = jnp.concatenate(
            [x_ref[:, :, pl.ds(pl.multiple_of((me ^ o) * width, width), width)] for o in offsets], axis=2
        )
    g_ref[...] = lax.dot_general(
        x.reshape(rows, x.shape[2]), kr, (((0,), (0,)), ((), ())), preferred_element_type=F32
    )


def load(offsets, x_hbm, a_hbm, b_hbm, c_hbm, x_ref, a_ref, b_ref, cb_ref, ga_ref, g_ref, sems):
    s_rows, rank = b_ref.shape
    r_rows = a_ref.shape[0]
    h_own = c_hbm.shape[0]
    width = g_ref.shape[0] // len(offsets)
    small = [
        pltpu.make_async_copy(a_hbm, a_ref, sems.at[0]),
        pltpu.make_async_copy(b_hbm, b_ref, sems.at[1]),
        pltpu.make_async_copy(c_hbm, cb_ref.at[pl.ds(0, h_own)], sems.at[2]),
        pltpu.make_async_copy(b_hbm, cb_ref.at[pl.ds(h_own, s_rows)], sems.at[3]),
    ]
    rows = r_rows // CHUNKS
    chunks = [
        pltpu.make_async_copy(x_hbm.at[pl.ds(i * rows, rows)], x_ref.at[pl.ds(i * rows, rows)], sems.at[4 + i])
        for i in range(CHUNKS)
    ]
    for copy in small + chunks:
        copy.start()
    for copy in small:
        copy.wait()
    ga_ref[...] = gram(a_ref[...])
    me = lax.axis_index("src")
    at = [pl.ds(pl.multiple_of((me ^ o) * width, width), width) for o in offsets]
    for i, copy in enumerate(chunks):
        mine = pl.ds(i * rows, rows)
        kr = (a_ref[mine][:, None, :] * b_ref[...][None]).reshape(rows * s_rows, rank)
        copy.wait()
        x = jnp.concatenate([x_ref[mine, :, a] for a in at], axis=2).reshape(rows * s_rows, 2 * width)
        part = lax.dot_general(x, kr, (((0,), (0,)), ((), ())), preferred_element_type=F32)
        g_ref[...] = part if i == 0 else g_ref[...] + part


def begin(o_ref):
    o_ref[...] = jnp.zeros_like(o_ref)


def products(a_in, b_in, t_ref, a_ref, b_ref, ga_ref):
    a_ref[...] = a_in[...]
    b_ref[...] = b_in[...]
    ga_ref[...] = gram(a_in[...])


def height_and_gram(offsets, x_ref, a_ref, b_ref, b1_ref, ga_ref, g_ref, hi_ref, lo_ref):
    hi_ref[...], lo_ref[...] = halves(ga_ref[...] * (gram(b_ref[...]) + gram(b1_ref[...])))
    height_terms(offsets, x_ref, a_ref, b_ref, g_ref)


def through(rows_ref, hi_ref, lo_ref):
    return sum(jnp.dot(rows_ref[...], part[...], preferred_element_type=F32) for part in (hi_ref, lo_ref))


def write_message(m_ref, *parts):
    top = functools.reduce(jnp.maximum, [column_top(part) for part in parts])
    e = exponent(top)
    scale = jnp.exp2(TOP - e)
    at = 0
    for part in parts:
        m_ref[at : at + part.shape[0]] = part * scale
        at += part.shape[0]
    m_ref[at:] = jnp.broadcast_to(e, (m_ref.shape[0] - at, e.shape[1]))


def meet(to_height, g_ref, in_ref, c2_ref, hi_ref, lo_ref, keep_ref, m_ref):
    h_own = keep_ref.shape[0]
    write_message(m_ref, (through(c2_ref, hi_ref, lo_ref) - (g_ref[h_own:] + in_ref[h_own:])) * to_height)
    keep_ref[...] = g_ref[0:h_own] + in_ref[0:h_own]


def combine(keep_ref, in_ref, ps_ref, m_ref):
    h_own = keep_ref.shape[0]
    share = keep_ref[...] + in_ref[0:h_own] * jnp.exp2(in_ref[h_own : h_own + 1] - TOP)
    write_message(m_ref, share, ps_ref[...])


def radius(to_radius, a_ref, b_ref, gc_ref, slab_ref, pa_ref):
    pa_ref[...] = (times(a_ref[...], gram(b_ref[...]) * gc_ref[...]) - slab_ref[...]) * to_radius


def project_four(
    to_height, to_source, x_ref, a_ref, b_ref, ga_ref, slab_ref, hi_ref, lo_ref, c0, c1, c2, c3,
    pa_ref, ps_ref, gc_ref, keep_ref, heights,
):
    s_rows, rank = b_ref.shape
    r_rows = a_ref.shape[0]
    h_own = c0.shape[0]
    me = lax.axis_index("src")
    for o, part in enumerate((c0, c1, c2, c3)):
        heights[pl.ds(pl.multiple_of((me ^ o) * h_own, h_own), h_own)] = part[...]
    x = x_ref[...].reshape(r_rows * s_rows, x_ref.shape[2])
    proj = jnp.dot(x, heights[...], preferred_element_type=F32).reshape(r_rows, s_rows, rank)
    pa_ref[...] = (proj * b_ref[...].astype(F32)[None]).sum(1)
    ps = (proj * a_ref[...].astype(F32)[:, None, :]).sum(0)
    keep_ref[...] = (through(c0, hi_ref, lo_ref) - slab_ref[...]) * to_height
    gc = gram(heights[...])
    gc_ref[...] = gc
    ps_ref[...] = (times(b_ref[...], ga_ref[...] * gc) - ps) * to_source


def local_four(slab, radius_factor, height_factor, source_factor, scales):
    r_rows, s_rows, width = slab.shape
    h_own, rank = height_factor.shape
    work = 2 * r_rows * s_rows * width * rank
    c2 = swap(height_factor, "src", 2)
    c3 = swap(height_factor, "src", 3)
    c1 = swap(height_factor, "src", 1)
    b1 = swap(source_factor, "src", 1)
    (tick,) = call(begin, [((8, LANES), F32)], (), 2 * work)
    a, b, ga = call(
        products,
        [((r_rows, rank), BF16), ((s_rows, rank), BF16), ((rank, rank), F32)],
        (radius_factor, source_factor, tick),
        work // 8,
        resident=False,
    )
    half, block = [((width // 2, rank), F32)], [((h_own, rank), F32)]
    (g_away,) = call(functools.partial(height_terms, (1, 3)), half, (slab, a, b), 2 * work, resident=False)
    g_in = swap(g_away, "src", 1)
    g_keep, hi, lo = call(
        functools.partial(height_and_gram, (0, 2)),
        half + [((rank, rank), BF16)] * 2,
        (slab, after(a, g_away), b, b1, ga),
        4 * work,
    )
    slab_part, away = call(
        functools.partial(meet, scales[1]),
        block + [((h_own + TAIL, rank), F32)],
        (g_keep, g_in, c2, hi, lo),
        work // 32,
    )
    away = away.astype(F16)
    share_in = swap(away, "src", 2)
    pa, ps, gc, keep = call(
        functools.partial(project_four, scales[1], scales[2]),
        [((r_rows, rank), F32), ((s_rows, rank), F32), ((rank, rank), F32)] + block,
        (slab, after(a, away), b, ga, slab_part, hi, lo, height_factor, c1, c2, c3),
        work,
        scratch=[pltpu.VMEM((width, rank), BF16)],
    )
    (m,) = call(combine, [((h_own + s_rows + TAIL, rank), F32)], (keep, share_in.astype(F32), ps), work // 32)
    m = m.astype(F16)
    (pa,) = call(
        functools.partial(radius, scales[0]), [((r_rows, rank), F32)], (a, b, gc, after(pa, m)), work // 32
    )
    return pa, m


def project(scales, n_src, x_ref, a_ref, b_ref, ga_ref, *refs):
    blocks, (pa_ref, ps_ref, ph_ref, heights) = refs[:n_src], refs[n_src:]
    s_rows, rank = b_ref.shape
    r_rows = a_ref.shape[0]
    h_own = blocks[0].shape[0] - s_rows
    me = lax.axis_index("src")
    for o, ref in enumerate(blocks):
        heights[pl.ds(pl.multiple_of((me ^ o) * h_own, h_own), h_own)] = ref[0:h_own]
    x = x_ref[...].reshape(r_rows * s_rows, x_ref.shape[2])
    proj = jnp.dot(x, heights[...], preferred_element_type=F32).reshape(r_rows, s_rows, rank)
    pa = (proj * b_ref[...].astype(F32)[None]).sum(1)
    ps = (proj * a_ref[...].astype(F32)[:, None, :]).sum(0)
    gb_own = gram(b_ref[...])
    gb = gb_own
    for ref in blocks[1:]:
        gb = gb + gram(ref[h_own:])
    gc = gram(heights[...])
    ga = ga_ref[...]
    to_radius, to_height, to_source = scales
    pa_ref[...] = (times(a_ref[...], gb_own * gc) - pa) * to_radius
    ps_ref[...] = (times(b_ref[...], ga * gc) - ps) * to_source
    ph_ref[...] = times(blocks[0][0:h_own], ga * gb) * to_height


def local_any(slab, radius_factor, height_factor, source_factor, scales):
    n_src = lax.axis_size("src")
    r_rows, s_rows, width = slab.shape
    h_own, rank = height_factor.shape
    work = 2 * r_rows * s_rows * width * rank
    src_bits = [1 << i for i in range(n_src.bit_length() - 1)]
    a, b, cb, ga = call(
        prepare,
        [((r_rows, rank), BF16), ((s_rows, rank), BF16), ((h_own + s_rows, rank), BF16), ((rank, rank), F32)],
        (radius_factor, source_factor, height_factor),
        work // 2,
        resident=False,
    )
    blocks = {0: cb}
    for bit in reversed(src_bits):
        blocks[bit] = swap(cb, "src", bit)
    if h_own % LANES == 0:
        offsets = list(range(n_src))
        (g_away,) = call(
            functools.partial(height_terms, offsets[1::2]), [((width // 2, rank), F32)], (slab, a, b), work // 2
        )
        g_in = swap(g_away, "src", 1)
        ready = after(a, g_away, *[blocks[bit] for bit in src_bits])
        (g_keep,) = call(
            functools.partial(height_terms, offsets[0::2]), [((width // 2, rank), F32)], (slab, ready, b), work // 2
        )
    else:
        (g,) = call(functools.partial(height_terms, None), [((width, rank), F32)], (slab, a, b), work)
        me = lax.axis_index("src")
        g = jnp.take(g.reshape(n_src, h_own, rank), me ^ jnp.arange(n_src), axis=0)
        g_away, g_keep = (g[i::2].reshape(width // 2, rank) for i in (1, 0))
        g_in = swap(g_away, "src", 1)
    for o in range(1, n_src):
        if o not in blocks:
            low = o & -o
            blocks[o] = swap(after(blocks[o ^ low], g_away), "src", low)
    g = g_keep + g_in
    for bit in src_bits[1:-1]:
        g = g.reshape(-1, 2, h_own, rank)
        g = (g[:, 0] + swap(g[:, 1], "src", bit)).reshape(-1, rank)
    share_in = swap(g[h_own:], "src", src_bits[-1])
    pa, ps, ph = call(
        functools.partial(project, scales, n_src),
        [((r_rows, rank), F32), ((s_rows, rank), F32), ((h_own, rank), F32)],
        (slab, a, b, ga, *[blocks[o] for o in range(n_src)]),
        work,
        scratch=[pltpu.VMEM((width, rank), BF16)],
    )
    ph = ph - (g[:h_own] + share_in) * scales[1]
    e = exponent(jnp.maximum(column_top(ph), column_top(ps)))
    return pa, pack(jnp.concatenate([ph, ps, jnp.zeros((TAIL, rank), F32)], axis=0), e)


def finish(v_ref, pa_ref, in_ref, r_ref, h_ref, s_ref):
    h_own = h_ref.shape[0]
    r_ref[...] = pa_ref[...] + in_ref[...]
    h_ref[...] = v_ref[0:h_own]
    s_ref[...] = v_ref[h_own : h_own + s_ref.shape[0]]


def pack(v, e):
    rows = lax.broadcasted_iota(jnp.int32, v.shape, 0)
    return jnp.where(rows < v.shape[0] - TAIL, v * jnp.exp2(TOP - e), e).astype(F16)


def unpack(m):
    e = m[-1:].astype(F32)
    return m.astype(F32) * jnp.exp2(e - TOP), e


def per_device(slab, radius_factor, height_factor, source_factor):
    n_rad, n_src = lax.axis_size("rad"), lax.axis_size("src")
    r_rows, s_rows, width = slab.shape
    h_own, rank = height_factor.shape
    total_r, total_s = r_rows * n_rad, s_rows * n_src
    scales = (
        (total_s * width) ** -0.5,
        (total_r * total_s) ** -0.5,
        (total_r * width) ** -0.5,
    )
    src_bits = [1 << i for i in range(n_src.bit_length() - 1)]
    rad_bits = [1 << i for i in range(n_rad.bit_length() - 1)]

    local = local_four if n_src == 4 and h_own % LANES == 0 else local_any
    pa, m = local(slab, radius_factor, height_factor, source_factor, scales)
    bits = src_bits[::-1]
    stages = [rad_bits[i : i + 2] for i in range(0, len(rad_bits), 2)]
    for i, stage in enumerate(stages):
        if len(stage) == 2:
            others = [sum(stage), stage[1], stage[0]]
        else:
            others = [stage[0] + (stage[0] // 2 if i else 0)]
        terms = [unpack(m)] + [unpack(swap(m, "rad", o)) for o in others]
        if len(bits) > 1:
            pa = after(pa, m)
            pa = pa + swap(pa, "src", bits.pop(0))
        values = [value for value, _ in terms]
        while len(values) > 1:
            values = [a + b for a, b in zip(values[0::2], values[1::2])]
        (v,) = values
        if i + 1 < len(stages):
            m = pack(v, functools.reduce(jnp.maximum, [x for _, x in terms]) + len(stage))
    while len(bits) > 1:
        pa = pa + swap(pa, "src", bits.pop(0))
    pa_in = swap(after(pa, m), "src", bits[0])
    return pl.pallas_call(
        finish,
        in_specs=[WHOLE] * 3,
        out_specs=[WHOLE] * 3,
        out_shape=[jax.ShapeDtypeStruct((rows, rank), F32) for rows in (r_rows, h_own, s_rows)],
    )(inside(v), inside(pa), inside(pa_in))


def solution(mesh):
    return jax.shard_map(
        per_device,
        mesh=mesh,
        in_specs=(P("rad", "src", None), P("rad", None), P("src", None), P("src", None)),
        out_specs=(P("rad", None), P("src", None), P("src", None)),
        check_vma=False,
    )
```

```python
import functools

import jax
import jax.numpy as jnp
from jax import lax
from jax.experimental import pallas as pl
from jax.experimental.pallas import tpu as pltpu
from jax.sharding import PartitionSpec as P

F32 = jnp.float32
BF16 = jnp.bfloat16
F16 = jnp.float16
VMEM_LIMIT = 32 * 1024 * 1024
LOAD_LIMIT = 54 * 1024 * 1024 + 512 * 1024
LANES = 128
CHUNKS = 8
TAIL = 8
TOP = 13.0
WHOLE = pl.BlockSpec(memory_space=pltpu.VMEM)


def inside(x):
    return pltpu.with_memory_space_constraint(x, pltpu.VMEM)


def after(x, *others):
    return lax.optimization_barrier((x, *others))[0]


def swap(x, axis, bit):
    return lax.ppermute(x, axis, [(i, i ^ bit) for i in range(lax.axis_size(axis))])


def call(body, outs, args, flops, resident=True, scratch=()):
    return pl.pallas_call(
        body,
        in_specs=[WHOLE] * len(args),
        out_specs=[WHOLE] * len(outs),
        out_shape=[pltpu.VMEM(shape, dtype) for shape, dtype in outs],
        scratch_shapes=scratch,
        compiler_params=pltpu.CompilerParams(vmem_limit_bytes=VMEM_LIMIT),
        cost_estimate=pl.CostEstimate(flops=flops, bytes_accessed=0, transcendentals=0),
    )(*[inside(a) if resident else a for a in args])


def gram(x):
    return lax.dot_general(x, x, (((0,), (0,)), ((), ())), preferred_element_type=F32)


def halves(m):
    hi = m.astype(BF16)
    return hi, (m - hi.astype(F32)).astype(BF16)


def times(x, m):
    hi, lo = halves(m)
    return jnp.dot(x, hi, preferred_element_type=F32) + jnp.dot(x, lo, preferred_element_type=F32)


def exponent(top):
    return jnp.clip(jnp.ceil(jnp.log2(jnp.maximum(top, 1e-30))), -100.0, 100.0)


def column_top(v):
    return jnp.max(jnp.abs(v), axis=0, keepdims=True)


def prepare(a_ref, b_ref, c_ref, a_out, b_out, cb_out, ga_out):
    h_own = c_ref.shape[0]
    cb_out[0:h_own] = c_ref[...]
    cb_out[h_own:] = b_ref[...]
    a_out[...] = a_ref[...]
    b_out[...] = b_ref[...]
    ga_out[...] = gram(a_ref[...])


def height_terms(offsets, x_ref, a_ref, b_ref, g_ref):
    s_rows, rank = b_ref.shape
    r_rows = a_ref.shape[0]
    rows = r_rows * s_rows
    kr = (a_ref[...][:, None, :] * b_ref[...][None]).reshape(rows, rank)
    if offsets is None:
        x = x_ref[...]
    else:
        width = g_ref.shape[0] // len(offsets)
        me = lax.axis_index("src")
        x = jnp.concatenate(
            [x_ref[:, :, pl.ds(pl.multiple_of((me ^ o) * width, width), width)] for o in offsets], axis=2
        )
    g_ref[...] = lax.dot_general(
        x.reshape(rows, x.shape[2]), kr, (((0,), (0,)), ((), ())), preferred_element_type=F32
    )


def load(offsets, x_hbm, a_hbm, b_hbm, c_hbm, x_ref, a_ref, b_ref, cb_ref, ga_ref, g_ref, sems):
    s_rows, rank = b_ref.shape
    r_rows = a_ref.shape[0]
    h_own = c_hbm.shape[0]
    width = g_ref.shape[0] // len(offsets)
    small = [
        pltpu.make_async_copy(a_hbm, a_ref, sems.at[0]),
        pltpu.make_async_copy(b_hbm, b_ref, sems.at[1]),
        pltpu.make_async_copy(c_hbm, cb_ref.at[pl.ds(0, h_own)], sems.at[2]),
        pltpu.make_async_copy(b_hbm, cb_ref.at[pl.ds(h_own, s_rows)], sems.at[3]),
    ]
    rows = r_rows // CHUNKS
    chunks = [
        pltpu.make_async_copy(x_hbm.at[pl.ds(i * rows, rows)], x_ref.at[pl.ds(i * rows, rows)], sems.at[4 + i])
        for i in range(CHUNKS)
    ]
    for copy in small + chunks:
        copy.start()
    for copy in small:
        copy.wait()
    ga_ref[...] = gram(a_ref[...])
    me = lax.axis_index("src")
    at = [pl.ds(pl.multiple_of((me ^ o) * width, width), width) for o in offsets]
    for i, copy in enumerate(chunks):
        mine = pl.ds(i * rows, rows)
        kr = (a_ref[mine][:, None, :] * b_ref[...][None]).reshape(rows * s_rows, rank)
        copy.wait()
        x = jnp.concatenate([x_ref[mine, :, a] for a in at], axis=2).reshape(rows * s_rows, 2 * width)
        part = lax.dot_general(x, kr, (((0,), (0,)), ((), ())), preferred_element_type=F32)
        g_ref[...] = part if i == 0 else g_ref[...] + part


def begin(o_ref):
    o_ref[...] = jnp.zeros_like(o_ref)


def products(a_in, b_in, t_ref, a_ref, b_ref, ga_ref):
    a_ref[...] = a_in[...]
    b_ref[...] = b_in[...]
    ga_ref[...] = gram(a_in[...])


def height_and_gram(offsets, x_ref, a_ref, b_ref, b1_ref, ga_ref, g_ref, hi_ref, lo_ref):
    hi_ref[...], lo_ref[...] = halves(ga_ref[...] * (gram(b_ref[...]) + gram(b1_ref[...])))
    height_terms(offsets, x_ref, a_ref, b_ref, g_ref)


def through(rows_ref, hi_ref, lo_ref):
    return sum(jnp.dot(rows_ref[...], part[...], preferred_element_type=F32) for part in (hi_ref, lo_ref))


def write_message(m_ref, *parts):
    top = functools.reduce(jnp.maximum, [column_top(part) for part in parts])
    e = exponent(top)
    scale = jnp.exp2(TOP - e)
    at = 0
    for part in parts:
        m_ref[at : at + part.shape[0]] = part * scale
        at += part.shape[0]
    m_ref[at:] = jnp.broadcast_to(e, (m_ref.shape[0] - at, e.shape[1]))


def meet(to_height, g_ref, in_ref, c2_ref, hi_ref, lo_ref, keep_ref, m_ref):
    h_own = keep_ref.shape[0]
    write_message(m_ref, (through(c2_ref, hi_ref, lo_ref) - (g_ref[h_own:] + in_ref[h_own:])) * to_height)
    keep_ref[...] = g_ref[0:h_own] + in_ref[0:h_own]


def combine(keep_ref, in_ref, ps_ref, m_ref):
    h_own = keep_ref.shape[0]
    share = keep_ref[...] + in_ref[0:h_own] * jnp.exp2(in_ref[h_own : h_own + 1] - TOP)
    write_message(m_ref, share, ps_ref[...])


def radius(to_radius, a_ref, b_ref, gc_ref, slab_ref, pa_ref):
    pa_ref[...] = (times(a_ref[...], gram(b_ref[...]) * gc_ref[...]) - slab_ref[...]) * to_radius


def project_four(
    to_height, to_source, x_ref, a_ref, b_ref, ga_ref, slab_ref, hi_ref, lo_ref, c0, c1, c2, c3,
    pa_ref, ps_ref, gc_ref, keep_ref, heights,
):
    s_rows, rank = b_ref.shape
    r_rows = a_ref.shape[0]
    h_own = c0.shape[0]
    me = lax.axis_index("src")
    for o, part in enumerate((c0, c1, c2, c3)):
        heights[pl.ds(pl.multiple_of((me ^ o) * h_own, h_own), h_own)] = part[...]
    x = x_ref[...].reshape(r_rows * s_rows, x_ref.shape[2])
    proj = jnp.dot(x, heights[...], preferred_element_type=F32).reshape(r_rows, s_rows, rank)
    pa_ref[...] = (proj * b_ref[...].astype(F32)[None]).sum(1)
    ps = (proj * a_ref[...].astype(F32)[:, None, :]).sum(0)
    keep_ref[...] = (through(c0, hi_ref, lo_ref) - slab_ref[...]) * to_height
    gc = gram(heights[...])
    gc_ref[...] = gc
    ps_ref[...] = (times(b_ref[...], ga_ref[...] * gc) - ps) * to_source


def local_four(slab, radius_factor, height_factor, source_factor, scales):
    r_rows, s_rows, width = slab.shape
    h_own, rank = height_factor.shape
    work = 2 * r_rows * s_rows * width * rank
    c2 = swap(height_factor, "src", 2)
    c3 = swap(height_factor, "src", 3)
    c1 = swap(height_factor, "src", 1)
    b1 = swap(source_factor, "src", 1)
    (tick,) = call(begin, [((8, LANES), F32)], (), 2 * work)
    a, b, ga = call(
        products,
        [((r_rows, rank), BF16), ((s_rows, rank), BF16), ((rank, rank), F32)],
        (radius_factor, source_factor, tick),
        work // 8,
        resident=False,
    )
    half, block = [((width // 2, rank), F32)], [((h_own, rank), F32)]
    (g_away,) = call(functools.partial(height_terms, (1, 3)), half, (slab, a, b), 2 * work, resident=False)
    g_in = swap(g_away, "src", 1)
    g_keep, hi, lo = call(
        functools.partial(height_and_gram, (0, 2)),
        half + [((rank, rank), BF16)] * 2,
        (slab, after(a, g_away), b, b1, ga),
        4 * work,
    )
    slab_part, away = call(
        functools.partial(meet, scales[1]),
        block + [((h_own + TAIL, rank), F32)],
        (g_keep, g_in, c2, hi, lo),
        work // 32,
    )
    away = away.astype(F16)
    share_in = swap(away, "src", 2)
    pa, ps, gc, keep = call(
        functools.partial(project_four, scales[1], scales[2]),
        [((r_rows, rank), F32), ((s_rows, rank), F32), ((rank, rank), F32)] + block,
        (slab, after(a, away), b, ga, slab_part, hi, lo, height_factor, c1, c2, c3),
        work,
        scratch=[pltpu.VMEM((width, rank), BF16)],
    )
    (m,) = call(combine, [((h_own + s_rows + TAIL, rank), F32)], (keep, share_in.astype(F32), ps), work // 32)
    m = m.astype(F16)
    (pa,) = call(
        functools.partial(radius, scales[0]), [((r_rows, rank), F32)], (a, b, gc, after(pa, m)), work // 32
    )
    return pa, m


def project(scales, n_src, x_ref, a_ref, b_ref, ga_ref, *refs):
    blocks, (pa_ref, ps_ref, ph_ref, heights) = refs[:n_src], refs[n_src:]
    s_rows, rank = b_ref.shape
    r_rows = a_ref.shape[0]
    h_own = blocks[0].shape[0] - s_rows
    me = lax.axis_index("src")
    for o, ref in enumerate(blocks):
        heights[pl.ds(pl.multiple_of((me ^ o) * h_own, h_own), h_own)] = ref[0:h_own]
    x = x_ref[...].reshape(r_rows * s_rows, x_ref.shape[2])
    proj = jnp.dot(x, heights[...], preferred_element_type=F32).reshape(r_rows, s_rows, rank)
    pa = (proj * b_ref[...].astype(F32)[None]).sum(1)
    ps = (proj * a_ref[...].astype(F32)[:, None, :]).sum(0)
    gb_own = gram(b_ref[...])
    gb = gb_own
    for ref in blocks[1:]:
        gb = gb + gram(ref[h_own:])
    gc = gram(heights[...])
    ga = ga_ref[...]
    to_radius, to_height, to_source = scales
    pa_ref[...] = (times(a_ref[...], gb_own * gc) - pa) * to_radius
    ps_ref[...] = (times(b_ref[...], ga * gc) - ps) * to_source
    ph_ref[...] = times(blocks[0][0:h_own], ga * gb) * to_height


def local_any(slab, radius_factor, height_factor, source_factor, scales):
    n_src = lax.axis_size("src")
    r_rows, s_rows, width = slab.shape
    h_own, rank = height_factor.shape
    work = 2 * r_rows * s_rows * width * rank
    src_bits = [1 << i for i in range(n_src.bit_length() - 1)]
    a, b, cb, ga = call(
        prepare,
        [((r_rows, rank), BF16), ((s_rows, rank), BF16), ((h_own + s_rows, rank), BF16), ((rank, rank), F32)],
        (radius_factor, source_factor, height_factor),
        work // 2,
        resident=False,
    )
    blocks = {0: cb}
    for bit in reversed(src_bits):
        blocks[bit] = swap(cb, "src", bit)
    if h_own % LANES == 0:
        offsets = list(range(n_src))
        (g_away,) = call(
            functools.partial(height_terms, offsets[1::2]), [((width // 2, rank), F32)], (slab, a, b), work // 2
        )
        g_in = swap(g_away, "src", 1)
        ready = after(a, g_away, *[blocks[bit] for bit in src_bits])
        (g_keep,) = call(
            functools.partial(height_terms, offsets[0::2]), [((width // 2, rank), F32)], (slab, ready, b), work // 2
        )
    else:
        (g,) = call(functools.partial(height_terms, None), [((width, rank), F32)], (slab, a, b), work)
        me = lax.axis_index("src")
        g = jnp.take(g.reshape(n_src, h_own, rank), me ^ jnp.arange(n_src), axis=0)
        g_away, g_keep = (g[i::2].reshape(width // 2, rank) for i in (1, 0))
        g_in = swap(g_away, "src", 1)
    for o in range(1, n_src):
        if o not in blocks:
            low = o & -o
            blocks[o] = swap(after(blocks[o ^ low], g_away), "src", low)
    g = g_keep + g_in
    for bit in src_bits[1:-1]:
        g = g.reshape(-1, 2, h_own, rank)
        g = (g[:, 0] + swap(g[:, 1], "src", bit)).reshape(-1, rank)
    share_in = swap(g[h_own:], "src", src_bits[-1])
    pa, ps, ph = call(
        functools.partial(project, scales, n_src),
        [((r_rows, rank), F32), ((s_rows, rank), F32), ((h_own, rank), F32)],
        (slab, a, b, ga, *[blocks[o] for o in range(n_src)]),
        work,
        scratch=[pltpu.VMEM((width, rank), BF16)],
    )
    ph = ph - (g[:h_own] + share_in) * scales[1]
    e = exponent(jnp.maximum(column_top(ph), column_top(ps)))
    return pa, pack(jnp.concatenate([ph, ps, jnp.zeros((TAIL, rank), F32)], axis=0), e)


def finish(v_ref, pa_ref, in_ref, r_ref, h_ref, s_ref):
    h_own = h_ref.shape[0]
    r_ref[...] = pa_ref[...] + in_ref[...]
    h_ref[...] = v_ref[0:h_own]
    s_ref[...] = v_ref[h_own : h_own + s_ref.shape[0]]


def pack(v, e):
    rows = lax.broadcasted_iota(jnp.int32, v.shape, 0)
    return jnp.where(rows < v.shape[0] - TAIL, v * jnp.exp2(TOP - e), e).astype(F16)


def unpack(m):
    e = m[-1:].astype(F32)
    return m.astype(F32) * jnp.exp2(e - TOP), e


def per_device(slab, radius_factor, height_factor, source_factor):
    n_rad, n_src = lax.axis_size("rad"), lax.axis_size("src")
    r_rows, s_rows, width = slab.shape
    h_own, rank = height_factor.shape
    total_r, total_s = r_rows * n_rad, s_rows * n_src
    scales = (
        (total_s * width) ** -0.5,
        (total_r * total_s) ** -0.5,
        (total_r * width) ** -0.5,
    )
    src_bits = [1 << i for i in range(n_src.bit_length() - 1)]
    rad_bits = [1 << i for i in range(n_rad.bit_length() - 1)]

    local = local_four if n_src == 4 and h_own % LANES == 0 else local_any
    pa, m = local(slab, radius_factor, height_factor, source_factor, scales)
    bits = src_bits[::-1]
    stages = [rad_bits[i : i + 2] for i in range(0, len(rad_bits), 2)][::-1]
    for i, stage in enumerate(stages):
        if len(stage) == 2:
            others = [sum(stage), stage[1], stage[0]]
        else:
            others = [stage[0] + stage[0] // 2]
        terms = [unpack(m)] + [unpack(swap(m, "rad", o)) for o in others]
        if len(bits) > 1:
            pa = after(pa, m)
            pa = pa + swap(pa, "src", bits.pop(0))
        values = [value for value, _ in terms]
        while len(values) > 1:
            values = [a + b for a, b in zip(values[0::2], values[1::2])]
        (v,) = values
        if i + 1 < len(stages):
            m = pack(v, functools.reduce(jnp.maximum, [x for _, x in terms]) + len(stage))
    while len(bits) > 1:
        pa = pa + swap(pa, "src", bits.pop(0))
    pa_in = swap(after(pa, m), "src", bits[0])
    return pl.pallas_call(
        finish,
        in_specs=[WHOLE] * 3,
        out_specs=[WHOLE] * 3,
        out_shape=[jax.ShapeDtypeStruct((rows, rank), F32) for rows in (r_rows, h_own, s_rows)],
    )(inside(v), inside(pa), inside(pa_in))


def solution(mesh):
    return jax.shard_map(
        per_device,
        mesh=mesh,
        in_specs=(P("rad", "src", None), P("rad", None), P("src", None), P("src", None)),
        out_specs=(P("rad", None), P("src", None), P("src", None)),
        check_vma=False,
    )
```

```python
import functools

import jax
import jax.numpy as jnp
from jax import lax
from jax.experimental import pallas as pl
from jax.experimental.pallas import tpu as pltpu
from jax.sharding import PartitionSpec as P

F32 = jnp.float32
BF16 = jnp.bfloat16
F16 = jnp.float16
VMEM_LIMIT = 32 * 1024 * 1024
LOAD_LIMIT = 54 * 1024 * 1024 + 512 * 1024
LANES = 128
CHUNKS = 8
TAIL = 8
TOP = 13.0
WHOLE = pl.BlockSpec(memory_space=pltpu.VMEM)


def inside(x):
    return pltpu.with_memory_space_constraint(x, pltpu.VMEM)


def after(x, *others):
    return lax.optimization_barrier((x, *others))[0]


def swap(x, axis, bit):
    return lax.ppermute(x, axis, [(i, i ^ bit) for i in range(lax.axis_size(axis))])


def call(body, outs, args, flops, resident=True, scratch=()):
    return pl.pallas_call(
        body,
        in_specs=[WHOLE] * len(args),
        out_specs=[WHOLE] * len(outs),
        out_shape=[pltpu.VMEM(shape, dtype) for shape, dtype in outs],
        scratch_shapes=scratch,
        compiler_params=pltpu.CompilerParams(vmem_limit_bytes=VMEM_LIMIT),
        cost_estimate=pl.CostEstimate(flops=flops, bytes_accessed=0, transcendentals=0),
    )(*[inside(a) if resident else a for a in args])


def gram(x):
    return lax.dot_general(x, x, (((0,), (0,)), ((), ())), preferred_element_type=F32)


def halves(m):
    hi = m.astype(BF16)
    return hi, (m - hi.astype(F32)).astype(BF16)


def times(x, m):
    hi, lo = halves(m)
    return jnp.dot(x, hi, preferred_element_type=F32) + jnp.dot(x, lo, preferred_element_type=F32)


def exponent(top):
    return jnp.clip(jnp.ceil(jnp.log2(jnp.maximum(top, 1e-30))), -100.0, 100.0)


def column_top(v):
    return jnp.max(jnp.abs(v), axis=0, keepdims=True)


def prepare(a_ref, b_ref, c_ref, a_out, b_out, cb_out, ga_out):
    h_own = c_ref.shape[0]
    cb_out[0:h_own] = c_ref[...]
    cb_out[h_own:] = b_ref[...]
    a_out[...] = a_ref[...]
    b_out[...] = b_ref[...]
    ga_out[...] = gram(a_ref[...])


def height_terms(offsets, x_ref, a_ref, b_ref, g_ref):
    s_rows, rank = b_ref.shape
    r_rows = a_ref.shape[0]
    rows = r_rows * s_rows
    kr = (a_ref[...][:, None, :] * b_ref[...][None]).reshape(rows, rank)
    if offsets is None:
        x = x_ref[...]
    else:
        width = g_ref.shape[0] // len(offsets)
        me = lax.axis_index("src")
        x = jnp.concatenate(
            [x_ref[:, :, pl.ds(pl.multiple_of((me ^ o) * width, width), width)] for o in offsets], axis=2
        )
    g_ref[...] = lax.dot_general(
        x.reshape(rows, x.shape[2]), kr, (((0,), (0,)), ((), ())), preferred_element_type=F32
    )


def load(offsets, x_hbm, a_hbm, b_hbm, c_hbm, x_ref, a_ref, b_ref, cb_ref, ga_ref, g_ref, sems):
    s_rows, rank = b_ref.shape
    r_rows = a_ref.shape[0]
    h_own = c_hbm.shape[0]
    width = g_ref.shape[0] // len(offsets)
    small = [
        pltpu.make_async_copy(a_hbm, a_ref, sems.at[0]),
        pltpu.make_async_copy(b_hbm, b_ref, sems.at[1]),
        pltpu.make_async_copy(c_hbm, cb_ref.at[pl.ds(0, h_own)], sems.at[2]),
        pltpu.make_async_copy(b_hbm, cb_ref.at[pl.ds(h_own, s_rows)], sems.at[3]),
    ]
    rows = r_rows // CHUNKS
    chunks = [
        pltpu.make_async_copy(x_hbm.at[pl.ds(i * rows, rows)], x_ref.at[pl.ds(i * rows, rows)], sems.at[4 + i])
        for i in range(CHUNKS)
    ]
    for copy in small + chunks:
        copy.start()
    for copy in small:
        copy.wait()
    ga_ref[...] = gram(a_ref[...])
    me = lax.axis_index("src")
    at = [pl.ds(pl.multiple_of((me ^ o) * width, width), width) for o in offsets]
    for i, copy in enumerate(chunks):
        mine = pl.ds(i * rows, rows)
        kr = (a_ref[mine][:, None, :] * b_ref[...][None]).reshape(rows * s_rows, rank)
        copy.wait()
        x = jnp.concatenate([x_ref[mine, :, a] for a in at], axis=2).reshape(rows * s_rows, 2 * width)
        part = lax.dot_general(x, kr, (((0,), (0,)), ((), ())), preferred_element_type=F32)
        g_ref[...] = part if i == 0 else g_ref[...] + part


def begin(o_ref):
    o_ref[...] = jnp.zeros_like(o_ref)


def products(a_in, b_in, t_ref, a_ref, b_ref, ga_ref):
    a_ref[...] = a_in[...]
    b_ref[...] = b_in[...]
    ga_ref[...] = gram(a_in[...])


def height_and_gram(offsets, x_ref, a_ref, b_ref, b1_ref, ga_ref, g_ref, hi_ref, lo_ref):
    hi_ref[...], lo_ref[...] = halves(ga_ref[...] * (gram(b_ref[...]) + gram(b1_ref[...])))
    height_terms(offsets, x_ref, a_ref, b_ref, g_ref)


def through(rows_ref, hi_ref, lo_ref):
    return sum(jnp.dot(rows_ref[...], part[...], preferred_element_type=F32) for part in (hi_ref, lo_ref))


def write_message(m_ref, *parts):
    top = functools.reduce(jnp.maximum, [column_top(part) for part in parts])
    e = exponent(top)
    scale = jnp.exp2(TOP - e)
    at = 0
    for part in parts:
        m_ref[at : at + part.shape[0]] = part * scale
        at += part.shape[0]
    m_ref[at:] = jnp.broadcast_to(e, (m_ref.shape[0] - at, e.shape[1]))


def partner_terms(c2_ref, hi_ref, lo_ref, out_ref):
    out_ref[...] = through(c2_ref, hi_ref, lo_ref)


def meet(to_height, g_ref, in_ref, gram_ref, keep_ref, m_ref):
    h_own = keep_ref.shape[0]
    write_message(m_ref, (gram_ref[...] - (g_ref[h_own:] + in_ref[h_own:])) * to_height)
    keep_ref[...] = g_ref[0:h_own] + in_ref[0:h_own]


def combine(keep_ref, in_ref, ps_ref, m_ref):
    h_own = keep_ref.shape[0]
    share = keep_ref[...] + in_ref[0:h_own] * jnp.exp2(in_ref[h_own : h_own + 1] - TOP)
    write_message(m_ref, share, ps_ref[...])


def radius(to_radius, a_ref, b_ref, gc_ref, slab_ref, pa_ref):
    pa_ref[...] = (times(a_ref[...], gram(b_ref[...]) * gc_ref[...]) - slab_ref[...]) * to_radius


def project_four(
    to_height, to_source, x_ref, a_ref, b_ref, ga_ref, slab_ref, hi_ref, lo_ref, c0, c1, c2, c3,
    pa_ref, ps_ref, gc_ref, keep_ref, heights,
):
    s_rows, rank = b_ref.shape
    r_rows = a_ref.shape[0]
    h_own = c0.shape[0]
    me = lax.axis_index("src")
    for o, part in enumerate((c0, c1, c2, c3)):
        heights[pl.ds(pl.multiple_of((me ^ o) * h_own, h_own), h_own)] = part[...]
    x = x_ref[...].reshape(r_rows * s_rows, x_ref.shape[2])
    proj = jnp.dot(x, heights[...], preferred_element_type=F32).reshape(r_rows, s_rows, rank)
    pa_ref[...] = (proj * b_ref[...].astype(F32)[None]).sum(1)
    ps = (proj * a_ref[...].astype(F32)[:, None, :]).sum(0)
    keep_ref[...] = (through(c0, hi_ref, lo_ref) - slab_ref[...]) * to_height
    gc = gram(heights[...])
    gc_ref[...] = gc
    ps_ref[...] = (times(b_ref[...], ga_ref[...] * gc) - ps) * to_source


def local_four(slab, radius_factor, height_factor, source_factor, scales):
    r_rows, s_rows, width = slab.shape
    h_own, rank = height_factor.shape
    work = 2 * r_rows * s_rows * width * rank
    c2 = swap(height_factor, "src", 2)
    c3 = swap(height_factor, "src", 3)
    c1 = swap(height_factor, "src", 1)
    b1 = swap(source_factor, "src", 1)
    (tick,) = call(begin, [((8, LANES), F32)], (), 2 * work)
    a, b, ga = call(
        products,
        [((r_rows, rank), BF16), ((s_rows, rank), BF16), ((rank, rank), F32)],
        (radius_factor, source_factor, tick),
        work // 8,
        resident=False,
    )
    half, block = [((width // 2, rank), F32)], [((h_own, rank), F32)]
    (g_away,) = call(functools.partial(height_terms, (1, 3)), half, (slab, a, b), 2 * work, resident=False)
    g_in = swap(g_away, "src", 1)
    g_keep, hi, lo = call(
        functools.partial(height_and_gram, (0, 2)),
        half + [((rank, rank), BF16)] * 2,
        (slab, after(a, g_away), b, b1, ga),
        4 * work,
    )
    (gram_part,) = call(partner_terms, block, (c2, hi, lo), work // 32)
    slab_part, away = call(
        functools.partial(meet, scales[1]),
        block + [((h_own + TAIL, rank), F32)],
        (g_keep, g_in, gram_part),
        work // 32,
    )
    away = away.astype(F16)
    share_in = swap(away, "src", 2)
    pa, ps, gc, keep = call(
        functools.partial(project_four, scales[1], scales[2]),
        [((r_rows, rank), F32), ((s_rows, rank), F32), ((rank, rank), F32)] + block,
        (slab, after(a, away), b, ga, slab_part, hi, lo, height_factor, c1, c2, c3),
        work,
        scratch=[pltpu.VMEM((width, rank), BF16)],
    )
    (m,) = call(combine, [((h_own + s_rows + TAIL, rank), F32)], (keep, share_in.astype(F32), ps), work // 32)
    m = m.astype(F16)
    (pa,) = call(
        functools.partial(radius, scales[0]), [((r_rows, rank), F32)], (a, b, gc, after(pa, m)), work // 32
    )
    return pa, m


def project(scales, n_src, x_ref, a_ref, b_ref, ga_ref, *refs):
    blocks, (pa_ref, ps_ref, ph_ref, heights) = refs[:n_src], refs[n_src:]
    s_rows, rank = b_ref.shape
    r_rows = a_ref.shape[0]
    h_own = blocks[0].shape[0] - s_rows
    me = lax.axis_index("src")
    for o, ref in enumerate(blocks):
        heights[pl.ds(pl.multiple_of((me ^ o) * h_own, h_own), h_own)] = ref[0:h_own]
    x = x_ref[...].reshape(r_rows * s_rows, x_ref.shape[2])
    proj = jnp.dot(x, heights[...], preferred_element_type=F32).reshape(r_rows, s_rows, rank)
    pa = (proj * b_ref[...].astype(F32)[None]).sum(1)
    ps = (proj * a_ref[...].astype(F32)[:, None, :]).sum(0)
    gb_own = gram(b_ref[...])
    gb = gb_own
    for ref in blocks[1:]:
        gb = gb + gram(ref[h_own:])
    gc = gram(heights[...])
    ga = ga_ref[...]
    to_radius, to_height, to_source = scales
    pa_ref[...] = (times(a_ref[...], gb_own * gc) - pa) * to_radius
    ps_ref[...] = (times(b_ref[...], ga * gc) - ps) * to_source
    ph_ref[...] = times(blocks[0][0:h_own], ga * gb) * to_height


def local_any(slab, radius_factor, height_factor, source_factor, scales):
    n_src = lax.axis_size("src")
    r_rows, s_rows, width = slab.shape
    h_own, rank = height_factor.shape
    work = 2 * r_rows * s_rows * width * rank
    src_bits = [1 << i for i in range(n_src.bit_length() - 1)]
    a, b, cb, ga = call(
        prepare,
        [((r_rows, rank), BF16), ((s_rows, rank), BF16), ((h_own + s_rows, rank), BF16), ((rank, rank), F32)],
        (radius_factor, source_factor, height_factor),
        work // 2,
        resident=False,
    )
    blocks = {0: cb}
    for bit in reversed(src_bits):
        blocks[bit] = swap(cb, "src", bit)
    if h_own % LANES == 0:
        offsets = list(range(n_src))
        (g_away,) = call(
            functools.partial(height_terms, offsets[1::2]), [((width // 2, rank), F32)], (slab, a, b), work // 2
        )
        g_in = swap(g_away, "src", 1)
        ready = after(a, g_away, *[blocks[bit] for bit in src_bits])
        (g_keep,) = call(
            functools.partial(height_terms, offsets[0::2]), [((width // 2, rank), F32)], (slab, ready, b), work // 2
        )
    else:
        (g,) = call(functools.partial(height_terms, None), [((width, rank), F32)], (slab, a, b), work)
        me = lax.axis_index("src")
        g = jnp.take(g.reshape(n_src, h_own, rank), me ^ jnp.arange(n_src), axis=0)
        g_away, g_keep = (g[i::2].reshape(width // 2, rank) for i in (1, 0))
        g_in = swap(g_away, "src", 1)
    for o in range(1, n_src):
        if o not in blocks:
            low = o & -o
            blocks[o] = swap(after(blocks[o ^ low], g_away), "src", low)
    g = g_keep + g_in
    for bit in src_bits[1:-1]:
        g = g.reshape(-1, 2, h_own, rank)
        g = (g[:, 0] + swap(g[:, 1], "src", bit)).reshape(-1, rank)
    share_in = swap(g[h_own:], "src", src_bits[-1])
    pa, ps, ph = call(
        functools.partial(project, scales, n_src),
        [((r_rows, rank), F32), ((s_rows, rank), F32), ((h_own, rank), F32)],
        (slab, a, b, ga, *[blocks[o] for o in range(n_src)]),
        work,
        scratch=[pltpu.VMEM((width, rank), BF16)],
    )
    ph = ph - (g[:h_own] + share_in) * scales[1]
    e = exponent(jnp.maximum(column_top(ph), column_top(ps)))
    return pa, pack(jnp.concatenate([ph, ps, jnp.zeros((TAIL, rank), F32)], axis=0), e)


def finish(v_ref, pa_ref, in_ref, r_ref, h_ref, s_ref):
    h_own = h_ref.shape[0]
    r_ref[...] = pa_ref[...] + in_ref[...]
    h_ref[...] = v_ref[0:h_own]
    s_ref[...] = v_ref[h_own : h_own + s_ref.shape[0]]


def pack(v, e):
    rows = lax.broadcasted_iota(jnp.int32, v.shape, 0)
    return jnp.where(rows < v.shape[0] - TAIL, v * jnp.exp2(TOP - e), e).astype(F16)


def unpack(m):
    e = m[-1:].astype(F32)
    return m.astype(F32) * jnp.exp2(e - TOP), e


def per_device(slab, radius_factor, height_factor, source_factor):
    n_rad, n_src = lax.axis_size("rad"), lax.axis_size("src")
    r_rows, s_rows, width = slab.shape
    h_own, rank = height_factor.shape
    total_r, total_s = r_rows * n_rad, s_rows * n_src
    scales = (
        (total_s * width) ** -0.5,
        (total_r * total_s) ** -0.5,
        (total_r * width) ** -0.5,
    )
    src_bits = [1 << i for i in range(n_src.bit_length() - 1)]
    rad_bits = [1 << i for i in range(n_rad.bit_length() - 1)]

    local = local_four if n_src == 4 and h_own % LANES == 0 else local_any
    pa, m = local(slab, radius_factor, height_factor, source_factor, scales)
    bits = src_bits[::-1]
    stages = [rad_bits[i : i + 2] for i in range(0, len(rad_bits), 2)]
    for i, stage in enumerate(stages):
        if len(stage) == 2:
            others = [sum(stage), stage[1], stage[0]]
        else:
            others = [stage[0] + (stage[0] // 2 if i else 0)]
        terms = [unpack(m)] + [unpack(swap(m, "rad", o)) for o in others]
        if len(bits) > 1:
            pa = after(pa, m)
            pa = pa + swap(pa, "src", bits.pop(0))
        values = [value for value, _ in terms]
        while len(values) > 1:
            values = [a + b for a, b in zip(values[0::2], values[1::2])]
        (v,) = values
        if i + 1 < len(stages):
            m = pack(v, functools.reduce(jnp.maximum, [x for _, x in terms]) + len(stage))
    while len(bits) > 1:
        pa = pa + swap(pa, "src", bits.pop(0))
    pa_in = swap(after(pa, m), "src", bits[0])
    return pl.pallas_call(
        finish,
        in_specs=[WHOLE] * 3,
        out_specs=[WHOLE] * 3,
        out_shape=[jax.ShapeDtypeStruct((rows, rank), F32) for rows in (r_rows, h_own, s_rows)],
    )(inside(v), inside(pa), inside(pa_in))


def solution(mesh):
    return jax.shard_map(
        per_device,
        mesh=mesh,
        in_specs=(P("rad", "src", None), P("rad", None), P("src", None), P("src", None)),
        out_specs=(P("rad", None), P("src", None), P("src", None)),
        check_vma=False,
    )
```

```python
import functools

import jax
import jax.numpy as jnp
from jax import lax
from jax.experimental import pallas as pl
from jax.experimental.pallas import tpu as pltpu
from jax.sharding import PartitionSpec as P

F32 = jnp.float32
BF16 = jnp.bfloat16
F16 = jnp.float16
VMEM_LIMIT = 32 * 1024 * 1024
LOAD_LIMIT = 54 * 1024 * 1024 + 512 * 1024
LANES = 128
CHUNKS = 8
TAIL = 8
TOP = 13.0
WHOLE = pl.BlockSpec(memory_space=pltpu.VMEM)


def inside(x):
    return pltpu.with_memory_space_constraint(x, pltpu.VMEM)


def after(x, *others):
    return lax.optimization_barrier((x, *others))[0]


def swap(x, axis, bit):
    return lax.ppermute(x, axis, [(i, i ^ bit) for i in range(lax.axis_size(axis))])


def call(body, outs, args, flops, resident=True, scratch=()):
    return pl.pallas_call(
        body,
        in_specs=[WHOLE] * len(args),
        out_specs=[WHOLE] * len(outs),
        out_shape=[pltpu.VMEM(shape, dtype) for shape, dtype in outs],
        scratch_shapes=scratch,
        compiler_params=pltpu.CompilerParams(vmem_limit_bytes=VMEM_LIMIT),
        cost_estimate=pl.CostEstimate(flops=flops, bytes_accessed=0, transcendentals=0),
    )(*[inside(a) if resident else a for a in args])


def gram(x):
    return lax.dot_general(x, x, (((0,), (0,)), ((), ())), preferred_element_type=F32)


def halves(m):
    hi = m.astype(BF16)
    return hi, (m - hi.astype(F32)).astype(BF16)


def times(x, m):
    hi, lo = halves(m)
    return jnp.dot(x, hi, preferred_element_type=F32) + jnp.dot(x, lo, preferred_element_type=F32)


def exponent(top):
    return jnp.clip(jnp.ceil(jnp.log2(jnp.maximum(top, 1e-30))), -100.0, 100.0)


def column_top(v):
    return jnp.max(jnp.abs(v), axis=0, keepdims=True)


def prepare(a_ref, b_ref, c_ref, a_out, b_out, cb_out, ga_out):
    h_own = c_ref.shape[0]
    cb_out[0:h_own] = c_ref[...]
    cb_out[h_own:] = b_ref[...]
    a_out[...] = a_ref[...]
    b_out[...] = b_ref[...]
    ga_out[...] = gram(a_ref[...])


def height_terms(offsets, x_ref, a_ref, b_ref, g_ref):
    s_rows, rank = b_ref.shape
    r_rows = a_ref.shape[0]
    rows = r_rows * s_rows
    kr = (a_ref[...][:, None, :] * b_ref[...][None]).reshape(rows, rank)
    if offsets is None:
        x = x_ref[...]
    else:
        width = g_ref.shape[0] // len(offsets)
        me = lax.axis_index("src")
        x = jnp.concatenate(
            [x_ref[:, :, pl.ds(pl.multiple_of((me ^ o) * width, width), width)] for o in offsets], axis=2
        )
    g_ref[...] = lax.dot_general(
        x.reshape(rows, x.shape[2]), kr, (((0,), (0,)), ((), ())), preferred_element_type=F32
    )


def load(offsets, x_hbm, a_hbm, b_hbm, c_hbm, x_ref, a_ref, b_ref, cb_ref, ga_ref, g_ref, sems):
    s_rows, rank = b_ref.shape
    r_rows = a_ref.shape[0]
    h_own = c_hbm.shape[0]
    width = g_ref.shape[0] // len(offsets)
    small = [
        pltpu.make_async_copy(a_hbm, a_ref, sems.at[0]),
        pltpu.make_async_copy(b_hbm, b_ref, sems.at[1]),
        pltpu.make_async_copy(c_hbm, cb_ref.at[pl.ds(0, h_own)], sems.at[2]),
        pltpu.make_async_copy(b_hbm, cb_ref.at[pl.ds(h_own, s_rows)], sems.at[3]),
    ]
    rows = r_rows // CHUNKS
    chunks = [
        pltpu.make_async_copy(x_hbm.at[pl.ds(i * rows, rows)], x_ref.at[pl.ds(i * rows, rows)], sems.at[4 + i])
        for i in range(CHUNKS)
    ]
    for copy in small + chunks:
        copy.start()
    for copy in small:
        copy.wait()
    ga_ref[...] = gram(a_ref[...])
    me = lax.axis_index("src")
    at = [pl.ds(pl.multiple_of((me ^ o) * width, width), width) for o in offsets]
    for i, copy in enumerate(chunks):
        mine = pl.ds(i * rows, rows)
        kr = (a_ref[mine][:, None, :] * b_ref[...][None]).reshape(rows * s_rows, rank)
        copy.wait()
        x = jnp.concatenate([x_ref[mine, :, a] for a in at], axis=2).reshape(rows * s_rows, 2 * width)
        part = lax.dot_general(x, kr, (((0,), (0,)), ((), ())), preferred_element_type=F32)
        g_ref[...] = part if i == 0 else g_ref[...] + part


def begin(o_ref):
    o_ref[...] = jnp.zeros_like(o_ref)


def products(a_in, b_in, t_ref, a_ref, b_ref, ga_ref):
    a_ref[...] = a_in[...]
    b_ref[...] = b_in[...]
    ga_ref[...] = gram(a_in[...])


def height_and_gram(offsets, x_ref, a_ref, b_ref, b1_ref, ga_ref, g_ref, hi_ref, lo_ref):
    hi_ref[...], lo_ref[...] = halves(ga_ref[...] * (gram(b_ref[...]) + gram(b1_ref[...])))
    height_terms(offsets, x_ref, a_ref, b_ref, g_ref)


def through(rows_ref, hi_ref, lo_ref):
    return sum(jnp.dot(rows_ref[...], part[...], preferred_element_type=F32) for part in (hi_ref, lo_ref))


def write_message(m_ref, *parts):
    top = functools.reduce(jnp.maximum, [column_top(part) for part in parts])
    e = exponent(top)
    scale = jnp.exp2(TOP - e)
    at = 0
    for part in parts:
        m_ref[at : at + part.shape[0]] = part * scale
        at += part.shape[0]
    m_ref[at:] = jnp.broadcast_to(e, (m_ref.shape[0] - at, e.shape[1]))


def meet(to_height, g_ref, in_ref, c2_ref, hi_ref, lo_ref, keep_ref, m_ref):
    h_own = keep_ref.shape[0]
    write_message(m_ref, (through(c2_ref, hi_ref, lo_ref) - (g_ref[h_own:] + in_ref[h_own:])) * to_height)
    keep_ref[...] = g_ref[0:h_own] + in_ref[0:h_own]


def combine(keep_ref, in_ref, ps_ref, m_ref):
    h_own = keep_ref.shape[0]
    share = keep_ref[...] + in_ref[0:h_own] * jnp.exp2(in_ref[h_own : h_own + 1] - TOP)
    write_message(m_ref, share, ps_ref[...])


def radius(to_radius, a_ref, b_ref, gc_ref, slab_ref, pa_ref):
    pa_ref[...] = (times(a_ref[...], gram(b_ref[...]) * gc_ref[...]) - slab_ref[...]) * to_radius


def project_four(
    to_height, to_source, x_ref, a_ref, b_ref, ga_ref, slab_ref, hi_ref, lo_ref, c0, c1, c2, c3,
    pa_ref, ps_ref, gc_ref, keep_ref, heights,
):
    s_rows, rank = b_ref.shape
    r_rows = a_ref.shape[0]
    h_own = c0.shape[0]
    me = lax.axis_index("src")
    for o, part in zip((0, 3, 2, 1), (c0, c1, c2, c3)):
        heights[pl.ds(pl.multiple_of((me ^ o) * h_own, h_own), h_own)] = part[...]
    x = x_ref[...].reshape(r_rows * s_rows, x_ref.shape[2])
    proj = jnp.dot(x, heights[...], preferred_element_type=F32).reshape(r_rows, s_rows, rank)
    pa_ref[...] = (proj * b_ref[...].astype(F32)[None]).sum(1)
    ps = (proj * a_ref[...].astype(F32)[:, None, :]).sum(0)
    keep_ref[...] = (through(c0, hi_ref, lo_ref) - slab_ref[...]) * to_height
    gc = gram(heights[...])
    gc_ref[...] = gc
    ps_ref[...] = (times(b_ref[...], ga_ref[...] * gc) - ps) * to_source


def local_four(slab, radius_factor, height_factor, source_factor, scales):
    r_rows, s_rows, width = slab.shape
    h_own, rank = height_factor.shape
    work = 2 * r_rows * s_rows * width * rank
    c2 = swap(height_factor, "src", 2)
    c3 = swap(height_factor, "src", 3)
    c1 = swap(height_factor, "src", 1)
    b1 = swap(source_factor, "src", 1)
    (tick,) = call(begin, [((8, LANES), F32)], (), 2 * work)
    a, b, ga = call(
        products,
        [((r_rows, rank), BF16), ((s_rows, rank), BF16), ((rank, rank), F32)],
        (radius_factor, source_factor, tick),
        work // 8,
        resident=False,
    )
    half, block = [((width // 2, rank), F32)], [((h_own, rank), F32)]
    (g_away,) = call(functools.partial(height_terms, (1, 3)), half, (slab, a, b), 2 * work, resident=False)
    g_in = swap(g_away, "src", 1)
    g_keep, hi, lo = call(
        functools.partial(height_and_gram, (0, 2)),
        half + [((rank, rank), BF16)] * 2,
        (slab, after(a, g_away), b, b1, ga),
        4 * work,
    )
    slab_part, away = call(
        functools.partial(meet, scales[1]),
        block + [((h_own + TAIL, rank), F32)],
        (g_keep, g_in, c2, hi, lo),
        work // 32,
    )
    away = away.astype(F16)
    share_in = swap(away, "src", 2)
    pa, ps, gc, keep = call(
        functools.partial(project_four, scales[1], scales[2]),
        [((r_rows, rank), F32), ((s_rows, rank), F32), ((rank, rank), F32)] + block,
        (slab, after(a, away), b, ga, slab_part, hi, lo, height_factor, c3, c2, c1),
        work,
        scratch=[pltpu.VMEM((width, rank), BF16)],
    )
    (m,) = call(combine, [((h_own + s_rows + TAIL, rank), F32)], (keep, share_in.astype(F32), ps), work // 32)
    m = m.astype(F16)
    (pa,) = call(
        functools.partial(radius, scales[0]), [((r_rows, rank), F32)], (a, b, gc, after(pa, m)), work // 32
    )
    return pa, m


def project(scales, n_src, x_ref, a_ref, b_ref, ga_ref, *refs):
    blocks, (pa_ref, ps_ref, ph_ref, heights) = refs[:n_src], refs[n_src:]
    s_rows, rank = b_ref.shape
    r_rows = a_ref.shape[0]
    h_own = blocks[0].shape[0] - s_rows
    me = lax.axis_index("src")
    for o, ref in enumerate(blocks):
        heights[pl.ds(pl.multiple_of((me ^ o) * h_own, h_own), h_own)] = ref[0:h_own]
    x = x_ref[...].reshape(r_rows * s_rows, x_ref.shape[2])
    proj = jnp.dot(x, heights[...], preferred_element_type=F32).reshape(r_rows, s_rows, rank)
    pa = (proj * b_ref[...].astype(F32)[None]).sum(1)
    ps = (proj * a_ref[...].astype(F32)[:, None, :]).sum(0)
    gb_own = gram(b_ref[...])
    gb = gb_own
    for ref in blocks[1:]:
        gb = gb + gram(ref[h_own:])
    gc = gram(heights[...])
    ga = ga_ref[...]
    to_radius, to_height, to_source = scales
    pa_ref[...] = (times(a_ref[...], gb_own * gc) - pa) * to_radius
    ps_ref[...] = (times(b_ref[...], ga * gc) - ps) * to_source
    ph_ref[...] = times(blocks[0][0:h_own], ga * gb) * to_height


def local_any(slab, radius_factor, height_factor, source_factor, scales):
    n_src = lax.axis_size("src")
    r_rows, s_rows, width = slab.shape
    h_own, rank = height_factor.shape
    work = 2 * r_rows * s_rows * width * rank
    src_bits = [1 << i for i in range(n_src.bit_length() - 1)]
    a, b, cb, ga = call(
        prepare,
        [((r_rows, rank), BF16), ((s_rows, rank), BF16), ((h_own + s_rows, rank), BF16), ((rank, rank), F32)],
        (radius_factor, source_factor, height_factor),
        work // 2,
        resident=False,
    )
    blocks = {0: cb}
    for bit in reversed(src_bits):
        blocks[bit] = swap(cb, "src", bit)
    if h_own % LANES == 0:
        offsets = list(range(n_src))
        (g_away,) = call(
            functools.partial(height_terms, offsets[1::2]), [((width // 2, rank), F32)], (slab, a, b), work // 2
        )
        g_in = swap(g_away, "src", 1)
        ready = after(a, g_away, *[blocks[bit] for bit in src_bits])
        (g_keep,) = call(
            functools.partial(height_terms, offsets[0::2]), [((width // 2, rank), F32)], (slab, ready, b), work // 2
        )
    else:
        (g,) = call(functools.partial(height_terms, None), [((width, rank), F32)], (slab, a, b), work)
        me = lax.axis_index("src")
        g = jnp.take(g.reshape(n_src, h_own, rank), me ^ jnp.arange(n_src), axis=0)
        g_away, g_keep = (g[i::2].reshape(width // 2, rank) for i in (1, 0))
        g_in = swap(g_away, "src", 1)
    for o in range(1, n_src):
        if o not in blocks:
            low = o & -o
            blocks[o] = swap(after(blocks[o ^ low], g_away), "src", low)
    g = g_keep + g_in
    for bit in src_bits[1:-1]:
        g = g.reshape(-1, 2, h_own, rank)
        g = (g[:, 0] + swap(g[:, 1], "src", bit)).reshape(-1, rank)
    share_in = swap(g[h_own:], "src", src_bits[-1])
    pa, ps, ph = call(
        functools.partial(project, scales, n_src),
        [((r_rows, rank), F32), ((s_rows, rank), F32), ((h_own, rank), F32)],
        (slab, a, b, ga, *[blocks[o] for o in range(n_src)]),
        work,
        scratch=[pltpu.VMEM((width, rank), BF16)],
    )
    ph = ph - (g[:h_own] + share_in) * scales[1]
    e = exponent(jnp.maximum(column_top(ph), column_top(ps)))
    return pa, pack(jnp.concatenate([ph, ps, jnp.zeros((TAIL, rank), F32)], axis=0), e)


def finish(v_ref, pa_ref, in_ref, r_ref, h_ref, s_ref):
    h_own = h_ref.shape[0]
    r_ref[...] = pa_ref[...] + in_ref[...]
    h_ref[...] = v_ref[0:h_own]
    s_ref[...] = v_ref[h_own : h_own + s_ref.shape[0]]


def pack(v, e):
    rows = lax.broadcasted_iota(jnp.int32, v.shape, 0)
    return jnp.where(rows < v.shape[0] - TAIL, v * jnp.exp2(TOP - e), e).astype(F16)


def unpack(m):
    e = m[-1:].astype(F32)
    return m.astype(F32) * jnp.exp2(e - TOP), e


def per_device(slab, radius_factor, height_factor, source_factor):
    n_rad, n_src = lax.axis_size("rad"), lax.axis_size("src")
    r_rows, s_rows, width = slab.shape
    h_own, rank = height_factor.shape
    total_r, total_s = r_rows * n_rad, s_rows * n_src
    scales = (
        (total_s * width) ** -0.5,
        (total_r * total_s) ** -0.5,
        (total_r * width) ** -0.5,
    )
    src_bits = [1 << i for i in range(n_src.bit_length() - 1)]
    rad_bits = [1 << i for i in range(n_rad.bit_length() - 1)]

    local = local_four if n_src == 4 and h_own % LANES == 0 else local_any
    pa, m = local(slab, radius_factor, height_factor, source_factor, scales)
    bits = src_bits[::-1]
    stages = [rad_bits[i : i + 2] for i in range(0, len(rad_bits), 2)]
    for i, stage in enumerate(stages):
        if len(stage) == 2:
            others = [sum(stage), stage[1], stage[0]]
        else:
            others = [stage[0] + (stage[0] // 2 if i else 0)]
        terms = [unpack(m)] + [unpack(swap(m, "rad", o)) for o in others]
        if len(bits) > 1:
            pa = after(pa, m)
            pa = pa + swap(pa, "src", bits.pop(0))
        values = [value for value, _ in terms]
        while len(values) > 1:
            values = [a + b for a, b in zip(values[0::2], values[1::2])]
        (v,) = values
        if i + 1 < len(stages):
            m = pack(v, functools.reduce(jnp.maximum, [x for _, x in terms]) + len(stage))
    while len(bits) > 1:
        pa = pa + swap(pa, "src", bits.pop(0))
    pa_in = swap(after(pa, m), "src", bits[0])
    return pl.pallas_call(
        finish,
        in_specs=[WHOLE] * 3,
        out_specs=[WHOLE] * 3,
        out_shape=[jax.ShapeDtypeStruct((rows, rank), F32) for rows in (r_rows, h_own, s_rows)],
    )(inside(v), inside(pa), inside(pa_in))


def solution(mesh):
    return jax.shard_map(
        per_device,
        mesh=mesh,
        in_specs=(P("rad", "src", None), P("rad", None), P("src", None), P("src", None)),
        out_specs=(P("rad", None), P("src", None), P("src", None)),
        check_vma=False,
    )
```
